32 devices in a mesh: seq: 8 (over y, x, core), tp: 4 (over z).
Axes of the slice: x: 2, y: 2, z: 4, core: 2. Of those that a mesh axis runs over, the one named last changes fastest.
Arguments:
- tokens: bfloat16 [1024, 16, 1024], P('seq', None, 'tp'), may hold values from -6 to 6
- norm_gain: bfloat16 [1024], P('tp'), may hold values from 0.5 to 1.5
- norm_shift: bfloat16 [1024], P('tp'), may hold values from -3 to 3
- query_weight: bfloat16 [1024, 1024], P(None, 'tp'), may hold values from -0.25 to 0.25
- key_weight: bfloat16 [1024, 1024], P(None, 'tp'), may hold values from -0.1875 to 0.1875
- value_weight: bfloat16 [1024, 1024], P(None, 'tp'), may hold values from -0.1875 to 0.1875
- output_weight: bfloat16 [1024, 1024], P('tp'), may hold values from -1 to 1
- inner_weight: bfloat16 [1024, 4096], P(None, 'tp'), may hold values from -0.1875 to 0.1875
- inner_bias: bfloat16 [4096], P('tp'), may hold values from -3 to 3
- outer_weight: bfloat16 [4096, 1024], P('tp'), may hold values from -0.09375 to 0.09375
- outer_bias: bfloat16 [1024], P('tp'), may hold values from -3 to 3
- lengths: int32 [16, 8], replicated, may hold values from 0 to 1024, as said below
- cotangent: bfloat16 [1024, 16, 1024], P('seq', None, 'tp'), may hold values from -6 to 6
Outputs:
- layer_out: bfloat16 [1024, 16, 1024], P('seq', None, 'tp')
- token_grad: float32 [1024, 16, 1024], P('seq', None, 'tp')
- gain_grad: float32 [1024], P('tp')
- shift_grad: float32 [1024], P('tp')
- query_weight_grad: float32 [1024, 1024], P(None, 'tp')
- key_weight_grad: float32 [1024, 1024], P(None, 'tp')
- value_weight_grad: float32 [1024, 1024], P(None, 'tp')
- output_weight_grad: float32 [1024, 1024], P('tp')
- inner_weight_grad: float32 [1024, 4096], P(None, 'tp')
- inner_bias_grad: float32 [4096], P('tp')
- outer_weight_grad: float32 [4096, 1024], P('tp')
- outer_bias_grad: float32 [1024], P('tp')
The draws below stay inside these ranges and needn't reach their ends.
Inputs may be any that keep to these rules, and one draw needn't show every extreme that they name: Each row holds its proteins one after another from position 0 and padding after them; the lengths of a row sum to at most 1024; in one row a single protein fills all 1024 positions.
All inputs are finite; a program needn't handle non-finite values.
Results may differ from the reference program's by a relative error of at most 0.012.
Values may be sent and summed in bfloat16 or wider, within the bound.
No kernel may reach another device: no remote copies, remote signals or barrier semaphores. Data moves between devices by JAX's collectives and lax.ppermute only.
A program may use at most 320 MiB of HBM per device.

```python
import jax
import jax.numpy as jnp
from jax import lax

MODEL_WIDTH = 1024
H = 16
DH = 64
FF = 4096
ROTARY = 32
PACKED_ROWS = 16
PROTEIN_SLOTS = 8
ROW_LENGTH = 1024


def draw_lengths(key, part):
    key = jax.random.fold_in(key, 11)
    leading_key, trailing_key, third_key = jax.random.split(key, 3)
    filled_count = jax.random.randint(leading_key, (PACKED_ROWS, 1), ROW_LENGTH // 2, ROW_LENGTH + 1)
    split_positions = jax.random.randint(trailing_key, (PACKED_ROWS, PROTEIN_SLOTS - 1), 0, ROW_LENGTH + 1)
    split_positions = jnp.sort(jnp.minimum(split_positions, filled_count), axis=1)
    bounds = jnp.concatenate([jnp.zeros((PACKED_ROWS, 1), jnp.int32), split_positions.astype(jnp.int32), filled_count.astype(jnp.int32)], axis=1)
    ragged = bounds[:, 1:] - bounds[:, :-1]
    full_row = jax.random.randint(third_key, (), 0, PACKED_ROWS)
    single_protein = jnp.where(jnp.arange(PROTEIN_SLOTS) == 0, ROW_LENGTH, 0).astype(jnp.int32)
    chosen = (jnp.arange(PACKED_ROWS) == full_row)[:, None]
    return jnp.where(chosen, single_protein[None, :], ragged).astype(jnp.int32)


def shard_levels(stream_key, shape, cuts, least, top_value):
    def one(axis_at, shards_of):
        draws = jax.random.uniform(jax.random.fold_in(jax.random.fold_in(stream_key, 6), axis_at), (shards_of,), jnp.float32, least / len(cuts), top_value / len(cuts))
        return jnp.repeat(jnp.exp(draws), shape[axis_at] // shards_of).reshape((-1,) + (1,) * (len(shape) - axis_at - 1))

    factor_of = one(*cuts[0])
    for cut in cuts[1:]:
        factor_of = factor_of * one(*cut)
    return factor_of


def noise(rng, dims, scale, limit, cuts=(), kind=jnp.bfloat16):
    values = scale * jax.random.normal(rng, dims, jnp.float32)
    if cuts:
        values = values * shard_levels(rng, dims, cuts, -0.22, 0.18)
    return jnp.clip(values, -limit, limit).astype(kind)


def setup_inputs(seed: int = 0) -> dict:
    seeds = jax.random.split(jax.random.key(seed), 14)
    return {
        "tokens": noise(seeds[0], (ROW_LENGTH, PACKED_ROWS, MODEL_WIDTH), 1.0, 6.0, ((0, 8), (2, 4))),
        "norm_gain": jnp.clip(1.0 + 0.1 * jax.random.normal(seeds[1], (MODEL_WIDTH,), jnp.float32), 0.5, 1.5).astype(jnp.bfloat16),
        "norm_shift": noise(seeds[2], (MODEL_WIDTH,), 0.5, 3.0, ((0, 4),)),
        "query_weight": noise(seeds[3], (MODEL_WIDTH, H * DH), (MODEL_WIDTH // 2) ** -0.5, 0.25, ((1, 4),)),
        "key_weight": noise(seeds[4], (MODEL_WIDTH, H * DH), MODEL_WIDTH ** -0.5, 0.1875, ((1, 4),)),
        "value_weight": noise(seeds[5], (MODEL_WIDTH, H * DH), MODEL_WIDTH ** -0.5, 0.1875, ((1, 4),)),
        "output_weight": noise(seeds[6], (H * DH, MODEL_WIDTH), (H * DH // 32) ** -0.5, 1.0, ((0, 4),)),
        "inner_weight": noise(seeds[7], (MODEL_WIDTH, FF), MODEL_WIDTH ** -0.5, 0.1875, ((1, 4),)),
        "inner_bias": noise(seeds[8], (FF,), 0.5, 3.0, ((0, 4),)),
        "outer_weight": noise(seeds[9], (FF, MODEL_WIDTH), FF ** -0.5, 0.09375, ((0, 4),)),
        "outer_bias": noise(seeds[10], (MODEL_WIDTH,), 0.5, 3.0, ((0, 4),)),
        "lengths": draw_lengths(jax.random.fold_in(seeds[13], 71), 0),
        "cotangent": noise(seeds[12], (ROW_LENGTH, PACKED_ROWS, MODEL_WIDTH), 1.0, 6.0, ((0, 8), (2, 4))),
    }


EPSILON = 1e-05
SCALING = 0.125
NEGATIVE = -1e+30
BASE_FREQ = 10000.0

@jax.custom_vjp
def low(v):
    return lax.optimization_barrier(v.astype(jnp.bfloat16)).astype(jnp.float32)

@jax.custom_vjp
def low_back(v):
    return v

def low_keep(v):
    return (low(v), None)

def low_pass(kept, grad):
    return (grad,)

def back_keep(v):
    return (v, None)

def back_low(kept, grad):
    return (low(grad),)
low.defvjp(low_keep, low_pass)
low_back.defvjp(back_keep, back_low)

def packing_plan(lengths, extent):
    protein_ends = jnp.cumsum(lengths, axis=1).astype(jnp.int32)
    places = jnp.arange(extent, dtype=jnp.int32)
    passed = protein_ends[:, None, :] <= places[None, :, None]
    protein_segment = lax.optimization_barrier(jnp.sum(passed.astype(jnp.int32), axis=2)).astype(jnp.int32)
    begins = lax.optimization_barrier(jnp.max(jnp.where(passed, protein_ends[:, None, :], 0), axis=2)).astype(jnp.int32)
    padded = places[None, :] >= protein_ends[:, -1:]
    protein_segment = jnp.where(padded, PROTEIN_SLOTS + 1 + places[None, :], protein_segment).astype(jnp.int32)
    inside_position = jnp.where(padded, 0, places[None, :] - begins).astype(jnp.int32)
    return (protein_segment, inside_position)

def angles(inside_position):
    dim_index = jnp.arange(DH, dtype=jnp.int32)
    halves = (dim_index // 2).astype(jnp.float32)
    frequency = jnp.where(dim_index < ROTARY, BASE_FREQ ** (-2.0 * halves / ROTARY), 0.0)
    phase_angle = inside_position.astype(jnp.float32)[..., None] * frequency
    return (jnp.cos(phase_angle), jnp.sin(phase_angle))

def pair_turn(values):
    paired = values.reshape(values.shape[:-1] + (values.shape[-1] // 2, 2))
    return jnp.stack([-paired[..., 1], paired[..., 0]], axis=-1).reshape(values.shape)

def rotate(values, cosine_table, sine_table):
    return values * cosine_table + pair_turn(values) * sine_table

def product(left, right):
    return jnp.dot(left, right, precision=lax.Precision.HIGHEST, preferred_element_type=jnp.float32)

def layer_row(params, row_in, protein_segment, inside_position):
    norm_gain, norm_shift, query_weight, key_weight, value_weight, output_weight, inner_weight, inner_bias, outer_weight, outer_bias = params
    extent = row_in.shape[0]
    centre = row_in - lax.optimization_barrier(jnp.mean(row_in, axis=-1, keepdims=True))
    spread = lax.optimization_barrier(jnp.mean(centre * centre, axis=-1, keepdims=True))
    normed = centre * lax.rsqrt(spread + EPSILON) * norm_gain + norm_shift
    hidden = low(normed)
    cosine_table, sine_table = angles(inside_position)
    cosine_table = cosine_table[:, None, :]
    sine_table = sine_table[:, None, :]
    queries = low_back(product(hidden, query_weight)).reshape(extent, H, DH)
    queries = low(rotate(queries, cosine_table, sine_table))
    key_heads = low_back(product(hidden, key_weight)).reshape(extent, H, DH)
    key_heads = low(rotate(key_heads, cosine_table, sine_table))
    values = low(low_back(product(hidden, value_weight))).reshape(extent, H, DH)
    query_span = min(512, extent)
    span_count = extent // query_span
    places = jnp.arange(extent, dtype=jnp.int32)

    def attend(entries):
        query_block, segment_block, place_block = entries
        scores = jnp.einsum('qhd,khd->hqk', query_block, key_heads, precision=lax.Precision.HIGHEST) * SCALING
        scores = low_back(scores)
        visible_mask = (segment_block[:, None] == protein_segment[None, :]) & (place_block[:, None] >= places[None, :])
        scores = jnp.where(visible_mask[None], scores, NEGATIVE)
        weights = jax.nn.softmax(scores, axis=-1)
        return jnp.einsum('hqk,khd->qhd', low(weights), values, precision=lax.Precision.HIGHEST)
    mixed = lax.map(jax.checkpoint(attend), (queries.reshape(span_count, query_span, H, DH), protein_segment.reshape(span_count, query_span), places.reshape(span_count, query_span)))
    mixed = low(low_back(mixed.reshape(extent, H * DH)))
    attention = product(mixed, output_weight)
    inner = low_back(product(hidden, inner_weight) + inner_bias)
    activated = low(jax.nn.gelu(inner, approximate=True))
    return row_in + attention + product(activated, outer_weight) + outer_bias

def reference(tokens, norm_gain, norm_shift, query_weight, key_weight, value_weight, output_weight, inner_weight, inner_bias, outer_weight, outer_bias, lengths, cotangent):
    params = tuple((weight.astype(jnp.float32) for weight in (norm_gain, norm_shift, query_weight, key_weight, value_weight, output_weight, inner_weight, inner_bias, outer_weight, outer_bias)))
    protein_segment, inside_position = packing_plan(lengths, ROW_LENGTH)
    rows_in = jnp.swapaxes(tokens.astype(jnp.float32), 0, 1)
    rows_back = jnp.swapaxes(cotangent.astype(jnp.float32), 0, 1)

    def advance(summed, entries):
        row_in, row_back, row_segment, row_within = entries

        def forward(weights, entry_row):
            return layer_row(weights, entry_row, row_segment, row_within)
        result, backward = jax.vjp(forward, params, row_in)
        weight_grads, entry_grad = backward(row_back)
        return (jax.tree.map(jnp.add, summed, weight_grads), (result, entry_grad))
    zero_grads = jax.tree.map(jnp.zeros_like, params)
    summed, outputs = lax.scan(advance, zero_grads, (rows_in, rows_back, protein_segment, inside_position))
    results, entry_grads = outputs
    return (jnp.swapaxes(results, 0, 1).astype(jnp.bfloat16), jnp.swapaxes(entry_grads, 0, 1), summed[0], summed[1], summed[2], summed[3], summed[4], summed[5], summed[6], summed[7], summed[8], summed[9])
```

```python
from functools import partial

import jax
import jax.numpy as jnp
from jax import lax
from jax.experimental import pallas as pl
from jax.experimental.pallas import tpu as pltpu
from jax.sharding import PartitionSpec as P

DH = 64
ROTARY = 32
PROTEIN_SLOTS = 8
LANES = 128

EPSILON = 1e-05
SCALING = 0.125
NEGATIVE = -1e30
BASE_FREQ = 10000.0
GELU_A = 0.7978845608028654
GELU_B = 0.044715

F32 = jnp.float32
BF16 = jnp.bfloat16
NT = (((1,), (1,)), ((), ()))
TN = (((0,), (0,)), ((), ()))
VMEM_LIMIT = 56 * 1024 * 1024


def behind(kernel, n_in, after, n_scalar=0):
    n_in = n_in + n_scalar

    def wrapped(*refs):
        return kernel(*refs[:n_in], *refs[n_in + len(after) :])

    return wrapped


def work(flops, bytes_accessed, times=3):
    return pl.CostEstimate(flops=times * flops, bytes_accessed=times * bytes_accessed, transcendentals=0)


def unused(after):
    return [pl.BlockSpec(memory_space=pl.ANY)] * len(after)


def params(**more):
    return pltpu.CompilerParams(vmem_limit_bytes=VMEM_LIMIT, **more)


def packing(lengths, extent):
    protein_ends = jnp.cumsum(lengths, axis=1)
    places = jnp.arange(extent, dtype=jnp.int32)
    passed = protein_ends[:, None, :] <= places[None, :, None]
    begins = jnp.max(jnp.where(passed, protein_ends[:, None, :], 0), axis=2)
    padded = places[None, :] >= protein_ends[:, -1:]
    starts = jnp.where(padded, places[None, :], begins)
    return starts, places[None, :] - starts


def turn_tables(inside_position):
    dim_index = jnp.arange(LANES, dtype=jnp.int32) % DH
    halves = (dim_index // 2).astype(F32)
    frequency = jnp.where(dim_index < ROTARY, BASE_FREQ ** (-2.0 * halves / ROTARY), 0.0)
    sign = jnp.where(dim_index % 2 == 0, -1.0, 1.0)
    phase_angle = inside_position.astype(F32)[..., None] * frequency
    return jnp.cos(phase_angle), jnp.sin(phase_angle) * sign


def swap_pairs(x):
    lane = lax.broadcasted_iota(jnp.int32, x.shape, 1)
    return jnp.where(lane % 2 == 0, pltpu.roll(x, LANES - 1, 1), pltpu.roll(x, 1, 1))


def norm_project_kernel(
    x_ref, gain_ref, shift_ref, wq_ref, wk_ref, wv_ref, win_ref, bias_ref, cos_ref, sin_ref,
    hidden_ref, qkv_ref, act_ref, slope_ref, stat_ref,
):
    parts, rows, part = x_ref.shape
    width = parts * part
    embed = wq_ref.shape[1]
    xs = [x_ref[k].astype(F32) for k in range(parts)]
    mean = sum(jnp.sum(x, axis=1, keepdims=True) for x in xs) * (1.0 / width)
    xs = [x - mean for x in xs]
    var = sum(jnp.sum(x * x, axis=1, keepdims=True) for x in xs) * (1.0 / width)
    inverse = lax.rsqrt(var + EPSILON)
    lane = lax.broadcasted_iota(jnp.int32, stat_ref.shape, 1)
    stat_ref[...] = jnp.where(lane == 0, mean, inverse)
    for k in range(parts):
        at = pl.ds(k * part, part)
        hidden_ref[:, at] = (xs[k] * inverse * gain_ref[:, at] + shift_ref[:, at]).astype(BF16)
    hidden = hidden_ref[...]
    cos, sin = cos_ref[...], sin_ref[...]
    for n, w_ref in enumerate((wq_ref, wk_ref)):
        pre = jnp.dot(hidden, w_ref[...], preferred_element_type=F32)
        for g in range(embed // LANES):
            one = pre[:, g * LANES : (g + 1) * LANES]
            qkv_ref[:, pl.ds(n * embed + g * LANES, LANES)] = (
                one * cos + swap_pairs(one) * sin
            ).astype(BF16)
    qkv_ref[:, pl.ds(2 * embed, embed)] = jnp.dot(
        hidden, wv_ref[...], preferred_element_type=F32
    ).astype(BF16)
    v = jnp.dot(hidden, win_ref[...], preferred_element_type=F32) + bias_ref[...]
    square = v * v
    t = jnp.tanh(GELU_A * v * (1.0 + GELU_B * square))
    act_ref[...] = (0.5 * v * (1.0 + t)).astype(BF16)
    slope_ref[...] = 0.5 * (1.0 + t) + 0.5 * v * (1.0 - t * t) * (
        GELU_A * (1.0 + 3.0 * GELU_B * square)
    )


def norm_project(x, gain, shift, wq, wk, wv, win, bias, cos, sin, after=()):
    parts, total, part = x.shape
    width, embed = wq.shape
    inner = win.shape[1]
    rows = min(256, total)
    whole = lambda i: (0, 0)
    block = lambda i: (i, 0)
    return pl.pallas_call(
        behind(norm_project_kernel, 10, after),
        grid=(total // rows,),
        in_specs=[
            pl.BlockSpec((parts, rows, part), lambda i: (0, i, 0)),
            pl.BlockSpec((1, width), whole),
            pl.BlockSpec((1, width), whole),
            pl.BlockSpec((width, embed), whole),
            pl.BlockSpec((width, embed), whole),
            pl.BlockSpec((width, embed), whole),
            pl.BlockSpec((width, inner), whole),
            pl.BlockSpec((1, inner), whole),
            pl.BlockSpec((rows, LANES), block),
            pl.BlockSpec((rows, LANES), block),
            *unused(after),
        ],
        out_specs=[
            pl.BlockSpec((rows, width), block),
            pl.BlockSpec((rows, 3 * embed), block),
            pl.BlockSpec((rows, inner), block),
            pl.BlockSpec((rows, inner), block),
            pl.BlockSpec((rows, LANES), block),
        ],
        out_shape=[
            jax.ShapeDtypeStruct((total, width), BF16),
            jax.ShapeDtypeStruct((total, 3 * embed), BF16),
            jax.ShapeDtypeStruct((total, inner), BF16),
            jax.ShapeDtypeStruct((total, inner), F32),
            jax.ShapeDtypeStruct((total, LANES), F32),
        ],
        compiler_params=params(),
        cost_estimate=work(2 * total * width * (3 * embed + inner), total * (4 * width + 6 * embed + 6 * inner)),
        name="norm_project",
    )(x, gain, shift, wq, wk, wv, win, bias, cos, sin, *after)


def push_back_kernel(c_ref, wo_ref, wout_ref, slope_ref, mixed_grad_ref, inner_grad_ref, bias_ref):
    parts, rows, part = c_ref.shape
    mixed_grad = inner = None
    for k in range(parts):
        at = pl.ds(k * part, part)
        one = jnp.dot(c_ref[k], wo_ref[at, :], preferred_element_type=F32)
        two = jnp.dot(c_ref[k], wout_ref[at, :], preferred_element_type=F32)
        mixed_grad = one if mixed_grad is None else mixed_grad + one
        inner = two if inner is None else inner + two
    mixed_grad_ref[...] = mixed_grad.astype(BF16)
    inner_low = (inner * slope_ref[...]).astype(BF16)
    inner_grad_ref[...] = inner_low

    @pl.when(pl.program_id(0) == 0)
    def _():
        bias_ref[...] = jnp.zeros_like(bias_ref)

    bias_ref[...] += jnp.sum(inner_low.astype(F32), axis=0, keepdims=True)


def push_back(c, wo, wout, slope, after=(), times=3):
    parts, total, part = c.shape
    width, embed = wo.shape
    inner = wout.shape[1]
    rows = min(512, total)
    whole = lambda i: (0, 0)
    block = lambda i: (i, 0)
    return pl.pallas_call(
        behind(push_back_kernel, 4, after),
        grid=(total // rows,),
        in_specs=[
            pl.BlockSpec((parts, rows, part), lambda i: (0, i, 0)),
            pl.BlockSpec((width, embed), whole),
            pl.BlockSpec((width, inner), whole),
            pl.BlockSpec((rows, inner), block),
            *unused(after),
        ],
        out_specs=[
            pl.BlockSpec((rows, embed), block),
            pl.BlockSpec((rows, inner), block),
            pl.BlockSpec((1, inner), whole),
        ],
        out_shape=[
            jax.ShapeDtypeStruct((total, embed), BF16),
            jax.ShapeDtypeStruct((total, inner), BF16),
            jax.ShapeDtypeStruct((1, inner), F32),
        ],
        compiler_params=params(),
        cost_estimate=work(2 * total * width * (embed + inner), total * (2 * width + 2 * embed + 6 * inner), times),
        name="push_back",
    )(c, wo, wout, slope, *after)


def attend_kernel(
    sizes, variant_ref, q_ref, k_ref, v_ref, g_ref, start_ref, cos_ref, sin_ref, out_ref, dk_ref, dv_ref
):
    at = pl.program_id(0)
    span, embed = q_ref.shape
    groups = [pl.ds(n * LANES, LANES) for n in range(embed // LANES)]
    first = lax.broadcasted_iota(jnp.int32, (span, LANES), 1) < DH
    row_at = pl.multiple_of(at * span, span)

    @pl.when(at == 0)
    def _():
        dk_ref[...] = jnp.zeros_like(dk_ref)
        dv_ref[...] = jnp.zeros_like(dv_ref)

    def unturn(x, cos, sin):
        return x * cos - swap_pairs(x) * sin

    def block(count):
        window = count * span
        base = pl.multiple_of(jnp.maximum(at + 1 - count, 0) * span, span)
        keys_at = pl.ds(base, window)
        rows = pl.ds(row_at, span)
        key_place = base + lax.broadcasted_iota(jnp.int32, (span, window), 1)
        query_place = row_at + lax.broadcasted_iota(jnp.int32, (span, window), 0)
        seen = (key_place >= start_ref[...]) & (key_place <= query_place)
        heads = []
        for group in groups:
            q = q_ref[:, group] * jnp.asarray(SCALING, BF16)
            g = g_ref[:, group]
            for mine in (first, jnp.logical_not(first)):
                heads.append((group, jnp.where(mine, q, jnp.zeros_like(q)), jnp.where(mine, g, jnp.zeros_like(g))))
        scores = [
            lax.dot_general(q, k_ref[keys_at, group], NT, preferred_element_type=F32) for group, q, g in heads
        ]
        pushed = [
            lax.dot_general(g, v_ref[keys_at, group], NT, preferred_element_type=F32) for group, q, g in heads
        ]
        weights = []
        for one in scores:
            one = jnp.where(seen, one, NEGATIVE)
            one = jnp.exp(one - jnp.max(one, axis=1, keepdims=True))
            weights.append(one * (1.0 / jnp.sum(one, axis=1, keepdims=True)))
        lows = [one.astype(BF16) for one in weights]
        grads = [
            (one * (push - jnp.sum(one * push, axis=1, keepdims=True))).astype(BF16)
            for one, push in zip(weights, pushed)
        ]
        for n, group in enumerate(groups):
            keys, values = k_ref[keys_at, group], v_ref[keys_at, group]
            pair = (2 * n, 2 * n + 1)
            mixed = [jnp.dot(lows[h], values, preferred_element_type=F32) for h in pair]
            dq = [jnp.dot(grads[h], keys, preferred_element_type=F32) for h in pair]
            dk_ref[keys_at, group] += sum(tn_dot(grads[h], heads[h][1]) for h in pair)
            dv_ref[keys_at, group] += sum(tn_dot(lows[h], heads[h][2]) for h in pair)
            out_ref[rows, group] = jnp.where(first, mixed[0], mixed[1]).astype(BF16)
            turned = jnp.where(first, dq[0], dq[1]) * SCALING
            out_ref[rows, pl.ds(embed + n * LANES, LANES)] = unturn(
                turned, cos_ref[rows, :], sin_ref[rows, :]
            ).astype(BF16)

    for n, count in enumerate(sizes):

        @pl.when(variant_ref[at] == n)
        def _(count=count):
            block(count)

    @pl.when(at == pl.num_programs(0) - 1)
    def _():
        for n, group in enumerate(groups):
            out_ref[:, pl.ds(2 * embed + n * LANES, LANES)] = unturn(
                dk_ref[:, group], cos_ref[...], sin_ref[...]
            ).astype(BF16)
            out_ref[:, pl.ds(3 * embed + n * LANES, LANES)] = dv_ref[:, group].astype(BF16)


def attend(qkv, g, starts, cos, sin, after=()):
    extent, embed = g.shape
    span = min(256, extent)
    spans = extent // span
    sizes = [size for size in range(1, spans) if size <= 4 or size % 2 == 0] + [spans]
    heads = starts.reshape(spans, span)[:, 0]
    need = jnp.arange(spans, dtype=jnp.int32) - heads // span + 1
    variant = jnp.sum((need[:, None] > jnp.asarray(sizes, jnp.int32)[None, :]).astype(jnp.int32), axis=1)
    spec = pl.BlockSpec
    return pl.pallas_call(
        behind(partial(attend_kernel, tuple(sizes)), 7, after, 1),
        grid_spec=pltpu.PrefetchScalarGridSpec(
            num_scalar_prefetch=1,
            grid=(spans,),
            in_specs=[
                spec((span, embed), lambda i, s: (i, 0)),
                spec((extent, embed), lambda i, s: (0, 1)),
                spec((extent, embed), lambda i, s: (0, 2)),
                spec((span, embed), lambda i, s: (i, 0)),
                spec((span, 1), lambda i, s: (i, 0)),
                spec((extent, LANES), lambda i, s: (0, 0)),
                spec((extent, LANES), lambda i, s: (0, 0)),
                *unused(after),
            ],
            out_specs=spec((extent, 4 * embed), lambda i, s: (0, 0)),
            scratch_shapes=[pltpu.VMEM((extent, embed), F32), pltpu.VMEM((extent, embed), F32)],
        ),
        out_shape=jax.ShapeDtypeStruct((extent, 4 * embed), BF16),
        compiler_params=params(),
        cost_estimate=work(12 * embed * extent * extent, extent * embed * 16),
        name="attend",
    )(variant, qkv, qkv, qkv, g, starts[:, None], cos, sin, *after)


def dense_back_kernel(
    back_ref, inner_ref, act_ref, x_ref, stat_ref, gain_ref, wqkv_ref, win_ref, wo_ref, wout_ref,
    out_ref, feature_ref, sums_ref,
):
    parts, rows, part = x_ref.shape
    extra = sums_ref.shape[0]
    total_rows = (out_ref.shape[1] - extra) // 2
    embed = wo_ref.shape[0]
    step = pl.program_id(0)
    mean, inverse = stat_ref[:, 0:1], stat_ref[:, 1:2]

    @pl.when(step == 0)
    def _():
        feature_ref[...] = jnp.zeros_like(feature_ref)
        sums_ref[...] = jnp.zeros_like(sums_ref)

    first = pl.ds(pl.multiple_of(step * rows, rows), rows)
    second = pl.ds(pl.multiple_of(total_rows + step * rows, rows), rows)
    ones = jnp.ones((8, LANES), BF16)
    one = two = None
    for k in range(parts):
        at = pl.ds(k * part, part)
        total = jnp.dot(inner_ref[...], win_ref[:, at], preferred_element_type=F32)
        total += jnp.dot(
            back_ref[:, pl.ds(embed, 3 * embed)], wqkv_ref[:, at], preferred_element_type=F32
        )
        out_ref[k, first, :] = total.astype(BF16)
        out_ref[k, second, :] = (
            jnp.dot(back_ref[:, pl.ds(0, embed)], wo_ref[:, at], preferred_element_type=F32)
            + jnp.dot(act_ref[...], wout_ref[:, at], preferred_element_type=F32)
        ).astype(BF16)
        scaled = (x_ref[k].astype(F32) - mean) * inverse
        product = total * scaled
        feature_ref[0:1, at] += jnp.sum(product, axis=0, keepdims=True)
        feature_ref[1:2, at] += jnp.sum(total, axis=0, keepdims=True)
        gain = gain_ref[:, at]
        for n in range(part // LANES):
            lanes = slice(n * LANES, (n + 1) * LANES)
            gained, moved = total[:, lanes] * gain[:, lanes], product[:, lanes] * gain[:, lanes]
            one = gained if one is None else one + gained
            two = moved if two is None else two + moved
    one, two = (
        lax.dot_general(ones, sums.astype(BF16), NT, preferred_element_type=F32) for sums in (one, two)
    )
    pieces = max(rows // part, 1)
    for start, row in ((0, one), (total_rows // part, two)):
        for n in range(pieces):
            sums_ref[pl.ds(start + step * pieces + n, 1), :] = row[0:1, n * part : (n + 1) * part]

    @pl.when(step == pl.num_programs(0) - 1)
    def _():
        for k in range(parts):
            out_ref[k, pl.ds(2 * total_rows, extra), :] = sums_ref[...].astype(BF16)


def extra_rows(total, part):
    return -(-2 * total // part // 16) * 16


def dense_back(back, inner_grad, act, x, stat, gain, wqkv, win, wo, wout, after=()):
    parts, total, part = x.shape
    embed, width = wo.shape
    inner = win.shape[0]
    rows = min(512, total)
    extra = extra_rows(total, part)
    whole = lambda i: (0, 0)
    block = lambda i: (i, 0)
    return pl.pallas_call(
        behind(dense_back_kernel, 10, after),
        grid=(total // rows,),
        in_specs=[
            pl.BlockSpec((rows, 4 * embed), block),
            pl.BlockSpec((rows, inner), block),
            pl.BlockSpec((rows, inner), block),
            pl.BlockSpec((parts, rows, part), lambda i: (0, i, 0)),
            pl.BlockSpec((rows, LANES), block),
            pl.BlockSpec((1, width), whole),
            pl.BlockSpec((3 * embed, width), whole),
            pl.BlockSpec((inner, width), whole),
            pl.BlockSpec((embed, width), whole),
            pl.BlockSpec((inner, width), whole),
            *unused(after),
        ],
        out_specs=[
            pl.BlockSpec((parts, 2 * total + extra, part), lambda i: (0, 0, 0)),
            pl.BlockSpec((2, width), whole),
        ],
        out_shape=[
            jax.ShapeDtypeStruct((parts, 2 * total + extra, part), BF16),
            jax.ShapeDtypeStruct((2, width), F32),
        ],
        scratch_shapes=[pltpu.VMEM((extra, part), F32)],
        compiler_params=params(),
        cost_estimate=work(2 * total * width * (4 * embed + 2 * inner), total * (6 * width + 8 * embed + 4 * inner)),
        name="dense_back",
    )(back, inner_grad, act, x, stat, gain, wqkv, win, wo, wout, *after)


def tn_dot(left, right):
    return lax.dot_general(left, right, TN, preferred_element_type=F32)


def piece_rows(shapes, devices):
    return [rows * columns // (devices * LANES) for rows, columns in shapes]


def grads_kernel(chunks, steps, n_in, n_total, n_small, carried, last, make, core_ref, *refs):
    at = chunks * n_in
    ins, small_refs, refs = refs[:at], refs[at : at + n_small], refs[at + n_small :]
    earlier, refs = refs[: n_total * carried], refs[n_total * carried :]
    if last:
        keep_ref, send_ref, *totals = refs
    else:
        totals = refs
    at = pl.program_id(0)

    @pl.when(at == 0)
    def _():
        for n, total in enumerate(totals):
            total[...] = earlier[n][...] if carried else jnp.zeros_like(total)

    for c in range(chunks):

        @pl.when(at // steps == c)
        def _(c=c):
            make(ins[c * n_in : (c + 1) * n_in], totals)

    if last:

        @pl.when(at == chunks * steps - 1)
        def _():
            chips = keep_ref.shape[0]
            for core, out_ref in ((core_ref[0], keep_ref), (1 - core_ref[0], send_ref)):
                for chip in range(chips):
                    offset = 0
                    for total in (*totals, *small_refs):
                        rows = total.shape[0] // (2 * chips)
                        start = pl.multiple_of((core * chips + chip) * rows, rows)
                        for n in range(total.shape[1] // LANES):
                            out_ref[chip, pl.ds(offset, rows), :] = total[
                                pl.ds(start, rows), pl.ds(n * LANES, LANES)
                            ].astype(BF16)
                            offset += rows


def feed_make(ins, totals):
    act, hidden, inner_grad, cot = ins
    outer_total, inner_total = totals
    parts, _, part = cot.shape
    left = act[...]
    for k in range(parts):
        outer_total[:, pl.ds(k * part, part)] += tn_dot(left, cot[k])
    inner_total[...] += tn_dot(hidden[...], inner_grad[...])


def head_make(ins, totals):
    back, hidden, cot = ins
    output_total, *projection_totals = totals
    parts, _, part = cot.shape
    embed = output_total.shape[0]
    left = back[:, pl.ds(0, embed)]
    for k in range(parts):
        output_total[:, pl.ds(k * part, part)] += tn_dot(left, cot[k])
    for n, total in enumerate(projection_totals):
        total[...] += tn_dot(hidden[...], back[:, pl.ds((n + 1) * embed, embed)])


def grads(make, shapes, name, core, devices, chunk_arrays, small=(), earlier=(), last=True, after=(), times=3):
    chunks = len(chunk_arrays)
    total = chunk_arrays[0][0].shape[0]
    rows = min(512, total)
    steps = total // rows
    specs, arrays = [], []
    for c, group in enumerate(chunk_arrays):
        pick = lambda i, c=c: jnp.clip(i - c * steps, 0, steps - 1)
        for array in group:
            if array.ndim == 2:
                specs.append(pl.BlockSpec((rows, array.shape[1]), lambda i, s, pick=pick: (pick(i), 0)))
            else:
                specs.append(
                    pl.BlockSpec((array.shape[0], rows, array.shape[2]), lambda i, s, pick=pick: (0, pick(i), 0))
                )
            arrays.append(array)
    for array in (*small, *earlier):
        specs.append(pl.BlockSpec(array.shape, lambda i, s: (0, 0)))
        arrays.append(array)
    packed = (devices // 2, sum(piece_rows((*shapes, *[a.shape for a in small]), devices)), LANES)
    if last:
        out_specs = [pl.BlockSpec(packed, lambda i, s: (0, 0, 0))] * 2
        out_shape = [jax.ShapeDtypeStruct(packed, BF16)] * 2
        scratch_shapes = [pltpu.VMEM(shape, F32) for shape in shapes]
    else:
        out_specs = [pl.BlockSpec(shape, lambda i, s: (0, 0)) for shape in shapes]
        out_shape = [jax.ShapeDtypeStruct(shape, F32) for shape in shapes]
        scratch_shapes = []
    kernel = partial(
        grads_kernel, chunks, steps, len(chunk_arrays[0]), len(shapes), len(small), len(earlier) > 0, last, make
    )
    return pl.pallas_call(
        behind(kernel, len(specs), after, 1),
        grid_spec=pltpu.PrefetchScalarGridSpec(
            num_scalar_prefetch=1,
            grid=(chunks * steps,),
            in_specs=specs + unused(after),
            out_specs=out_specs,
            scratch_shapes=scratch_shapes,
        ),
        out_shape=out_shape,
        compiler_params=params(),
        cost_estimate=work(
            sum(2 * chunks * total * a * b for a, b in shapes), 2 * sum(a.size for a in arrays), times
        ),
        name=name,
    )(core, *arrays, *after)


def fold_kernel(keep_ref, came_ref, out_ref):
    for n in range(keep_ref.shape[0]):
        out_ref[n] = (keep_ref[n].astype(F32) + came_ref[n].astype(F32)).astype(BF16)


def elementwise(kernel, name, arrays, shape=None, after=(), times=3):
    spec = pl.BlockSpec(memory_space=pltpu.VMEM)
    shape = arrays[0].shape if shape is None else shape
    return pl.pallas_call(
        behind(kernel, len(arrays), after),
        in_specs=[spec] * len(arrays) + unused(after),
        out_specs=spec,
        out_shape=jax.ShapeDtypeStruct(shape, BF16),
        compiler_params=params(),
        cost_estimate=work(3 * arrays[0].size, 6 * arrays[0].size, times),
        name=name,
    )(*arrays, *after)


def merge_kernel(pieces_ref, keep_ref, came_ref, out_ref):
    rows = pieces_ref.shape[1]
    total = pieces_ref[0].astype(F32)
    for n in range(1, pieces_ref.shape[0]):
        total += pieces_ref[n].astype(F32)
    total = total.astype(BF16)
    for n in range(out_ref.shape[0]):
        out_ref[n, pl.ds(0, rows), :] = total
        out_ref[n, pl.ds(rows, keep_ref.shape[1]), :] = (
            keep_ref[n].astype(F32) + came_ref[n].astype(F32)
        ).astype(BF16)


def add_kernel(skip, x_ref, out_ref):
    rows = pl.ds(skip, out_ref.shape[1])
    total = x_ref[0, rows, :].astype(F32)
    for n in range(1, x_ref.shape[0]):
        total += x_ref[n, rows, :].astype(F32)
    total = total.astype(BF16)
    for n in range(out_ref.shape[0]):
        out_ref[n] = total


def passed_on(array, after):
    spec = pl.BlockSpec(memory_space=pl.ANY)
    return pl.pallas_call(
        lambda *refs: None,
        in_specs=[spec] * (1 + len(after)),
        out_specs=spec,
        out_shape=jax.ShapeDtypeStruct(array.shape, array.dtype),
        input_output_aliases={0: 0},
        compiler_params=params(),
        name="passed_on",
    )(array, *after)


def unpack_kernel(n_out, core_ref, own_ref, other_ref, *refs):
    matrix_refs, vector_refs, small_refs = refs[:n_out], refs[n_out:], ()
    if len(refs) > n_out:
        vector_refs, small_refs = refs[n_out:-1], refs[-1:]
    chips = own_ref.shape[0]
    for core, ref in ((core_ref[0], own_ref), (1 - core_ref[0], other_ref)):
        for chip in range(chips):
            offset = 0
            for out_ref in (*matrix_refs, *small_refs):
                rows = out_ref.shape[0] // (2 * chips)
                start = pl.multiple_of((core * chips + chip) * rows, rows)
                for block in range(out_ref.shape[1] // LANES):
                    out_ref[pl.ds(start, rows), pl.ds(block * LANES, LANES)] = ref[
                        chip, pl.ds(offset, rows), :
                    ].astype(F32)
                    offset += rows
    row = 0
    for out_ref in vector_refs:
        for block in range(out_ref.shape[1] // LANES):
            out_ref[:, pl.ds(block * LANES, LANES)] = small_refs[0][pl.ds(row, 1), :]
            row += 1


def unpack(core, own, other, shapes, vectors=(), small_shape=None, after=()):
    spec = pl.BlockSpec(memory_space=pltpu.VMEM)
    outs = (*shapes, *[(1, size) for size in vectors])
    return pl.pallas_call(
        behind(partial(unpack_kernel, len(shapes)), 2, after, 1),
        in_specs=[pl.BlockSpec(memory_space=pltpu.SMEM), spec, spec] + unused(after),
        out_specs=[spec] * len(outs),
        out_shape=[jax.ShapeDtypeStruct(shape, F32) for shape in outs],
        scratch_shapes=[pltpu.VMEM(small_shape, F32)] if vectors else [],
        compiler_params=params(),
        cost_estimate=work(own.size, 12 * own.size),
        name="unpack",
    )(core, own, other, *after)


def last_step_kernel(chunks, width, *refs):
    both_refs, stat_refs, tok_refs, cot_refs = (refs[n * chunks : (n + 1) * chunks] for n in range(4))
    gain_ref, bias_ref, out_ref, grad_ref, plain_ref, columns_ref = refs[4 * chunks :]
    per, span, part = tok_refs[0].shape
    halves = part // LANES
    total = per * LANES
    step = pl.program_id(0)

    @pl.when(step == 0)
    def _():
        for c, both_ref in enumerate(both_refs):
            sums = both_ref[pl.ds(2 * total, both_ref.shape[0] - 2 * total), :]
            shape = (sums.shape[0], LANES)
            eye = lax.broadcasted_iota(jnp.int32, shape, 0) == lax.broadcasted_iota(jnp.int32, shape, 1)
            for h in range(halves):
                columns_ref[c * halves + h] = tn_dot(
                    sums[:, h * LANES : (h + 1) * LANES], eye.astype(F32).astype(BF16)
                ) * (1.0 / width)

    here = pl.ds(pl.multiple_of(step * span, span), span)
    for c, (both_ref, stat_ref, tok_ref, cot_ref) in enumerate(zip(both_refs, stat_refs, tok_refs, cot_refs)):
        for n in range(per):
            r = c * per + n
            at = n * LANES + step * span
            hidden_grad = both_ref[pl.ds(pl.multiple_of(at, span), span), :].astype(F32)
            branch = both_ref[pl.ds(pl.multiple_of(total + at, span), span), :].astype(F32)
            columns = columns_ref[c * halves + n % halves, here, :]
            first = columns[:, n // halves : n // halves + 1]
            second = columns[:, (per + n) // halves : (per + n) // halves + 1]
            mean, inverse = stat_ref[n, :, 0:1], stat_ref[n, :, 1:2]
            token = tok_ref[n].astype(F32)
            scaled = (token - mean) * inverse
            plain_ref[:, r, :] = token + branch + bias_ref[...]
            grad_ref[:, r, :] = cot_ref[n].astype(F32) + inverse * (
                hidden_grad * gain_ref[...] - first - scaled * second
            )
    out_ref[...] = plain_ref[...].astype(BF16)


def last_step(boths, stats, tokens, cotangents, gain, bias, width, positions):
    chunks = len(boths)
    total, part = tokens[0].shape
    per = total // positions
    rows = chunks * per
    in_rows = lambda array: array.reshape(per, positions, array.shape[1])
    span = min(32, positions)
    return pl.pallas_call(
        partial(last_step_kernel, chunks, width),
        grid=(positions // span,),
        in_specs=[
            *[pl.BlockSpec(both.shape, lambda i: (0, 0)) for both in boths],
            *[pl.BlockSpec((per, span, LANES), lambda i: (0, i, 0))] * chunks,
            *[pl.BlockSpec((per, span, part), lambda i: (0, i, 0))] * (2 * chunks),
            *[pl.BlockSpec((1, part), lambda i: (0, 0))] * 2,
        ],
        out_specs=[pl.BlockSpec((span, rows, part), lambda i: (i, 0, 0))] * 2,
        out_shape=[
            jax.ShapeDtypeStruct((positions, rows, part), BF16),
            jax.ShapeDtypeStruct((positions, rows, part), F32),
        ],
        scratch_shapes=[
            pltpu.VMEM((span, rows, part), F32),
            pltpu.VMEM((chunks * (part // LANES), LANES, LANES), F32),
        ],
        compiler_params=params(),
        cost_estimate=work(20 * total * part, 12 * total * part),
        name="last_step",
    )(*boths, *map(in_rows, (*stats, *tokens, *cotangents)), gain, bias)


def partner(array, axis, bit):
    size = lax.axis_size(axis)
    return lax.ppermute(array, axis, [(i, i ^ bit) for i in range(size)])


def to_chips(pieces, axis):
    size = lax.axis_size(axis)
    groups = [list(range(core, size, 2)) for core in range(2)]
    return lax.all_to_all(pieces, axis, 0, 0, tiled=True, axis_index_groups=groups)


def small_sum(array, axes):
    for axis in axes:
        bit = 1
        while bit < lax.axis_size(axis):
            array = array + partner(array, axis, bit)
            bit *= 2
    return array


def body(
    tokens, norm_gain, norm_shift, query_weight, key_weight, value_weight, output_weight,
    inner_weight, inner_bias, outer_weight, outer_bias, lengths, cotangent,
):
    shard_len, batch_rows, local_width = tokens.shape
    seq_count, tp_count = lax.axis_size("seq"), lax.axis_size("tp")
    position, width_index = lax.axis_index("seq"), lax.axis_index("tp")
    extent = shard_len * seq_count
    width, embed = query_weight.shape
    inner = inner_weight.shape[1]
    chunks = batch_rows // seq_count

    own_tokens, own_cotangent = (
        [part.reshape(extent, local_width) for part in jnp.split(jnp.swapaxes(array, 0, 1), chunks)]
        for array in (tokens, cotangent)
    )
    back_qkv = jnp.concatenate([w.T for w in (query_weight, key_weight, value_weight)], axis=0)
    back_inner, back_output, back_outer = inner_weight.T, output_weight.T, outer_weight.T
    token_parts = [lax.all_gather(own_tokens[c], "tp") for c in range(chunks)]
    cotangent_parts = [lax.all_gather(own_cotangent[c], "tp") for c in range(chunks)]
    vectors = lax.all_gather(jnp.stack([norm_gain, norm_shift]), "tp", axis=1, tiled=True)
    vectors = vectors.astype(F32)
    gain, shift = vectors[0:1], vectors[1:2]

    starts, places = packing(lengths, extent)
    own_places = lax.dynamic_slice_in_dim(places, position * shard_len, shard_len, 1)
    own_cos, own_sin = turn_tables(own_places.reshape(chunks, extent))
    row_starts = [lax.dynamic_index_in_dim(starts, c * seq_count + position, 0, False) for c in range(chunks)]
    row_places = [lax.dynamic_index_in_dim(places, c * seq_count + position, 0, False) for c in range(chunks)]
    row_tables = [turn_tables(row) for row in row_places]
    bias_row = inner_bias.astype(F32)[None]

    def exchange(array):
        split = array.reshape(seq_count, shard_len, array.shape[-1])
        return lax.all_to_all(split, "seq", 0, 0, tiled=True).reshape(extent, array.shape[-1])

    stages = [dict() for _ in range(chunks)]
    place = jnp.stack([position % 2, position // 2]).astype(jnp.int32)
    feed_shapes = ((inner, width), (width, inner))

    def project(c, after=()):
        o = stages[c]
        o["hidden"], qkv, o["act"], o["slope"], o["stat"] = norm_project(
            token_parts[c], gain, shift, query_weight, key_weight, value_weight, inner_weight,
            bias_row, own_cos[c], own_sin[c], after=after,
        )
        o["qkv_rows"] = exchange(qkv)

    def push(c, after=()):
        o = stages[c]
        mixed_grad, o["inner_grad"], o["bias"] = push_back(
            cotangent_parts[c], back_output, back_outer, o["slope"], after=after, times=20 if c else 3
        )
        o["grad_rows"] = exchange(mixed_grad)

    def feed_grads(c, earlier):
        o = stages[c]
        return tuple(
            grads(
                feed_make, feed_shapes, "feed_grads", place[:1], seq_count,
                [(o["act"], o["hidden"], o["inner_grad"], cotangent_parts[c])],
                earlier=earlier, last=c == chunks - 1,
            )
        )

    def mix(c, after=()):
        o = stages[c]
        o["attention"] = attend(o["qkv_rows"], o["grad_rows"], row_starts[c], *row_tables[c], after=after)
        o["back"] = exchange(o["attention"])

    def finish(c, after=()):
        o = stages[c]
        o["made"], o["feature"] = dense_back(
            o["back"], o["inner_grad"], o["act"], token_parts[c], o["stat"], gain, back_qkv, back_inner,
            output_weight, outer_weight, after=after,
        )
        o["both"] = lax.psum_scatter(o["made"], "tp", scatter_dimension=0)

    feed = ()
    for c in range(chunks):
        if c == 0:
            project(c)
            push(c, after=(stages[c]["qkv_rows"], back_qkv, back_inner))
        else:
            project(c, after=(stages[c - 1]["attention"],))
            finish(c - 1, after=(stages[c]["hidden"],))
            push(c, after=(stages[c - 1]["made"], stages[c]["qkv_rows"]))
        feed = feed_grads(c, feed)
        mix(c, after=feed)
    outs = stages

    def both(make):
        return sum(make(c, outs[c]) for c in range(chunks))

    last = stages[-1]
    feed = elementwise(fold_kernel, "fold", [feed[0], partner(feed[1], "seq", 1)], after=(last["attention"],))
    finish(chunks - 1, after=(feed,))
    feed = to_chips(feed, "seq")

    feature = small_sum(both(lambda c, o: o["feature"]).reshape(-1, LANES), ("tp",)).reshape(2, width)
    feature = lax.dynamic_slice_in_dim(feature, width_index * local_width, local_width, 1)
    small = jnp.concatenate(
        [
            feature.reshape(-1), both(lambda c, o: o["bias"])[0],
            jnp.sum(cotangent.astype(F32), axis=(0, 1)),
        ]
    )
    small_shape = (seq_count * 16, LANES)
    small = jnp.pad(small, (0, small_shape[0] * LANES - small.size)).reshape(small_shape)
    head_shapes = ((embed, width), (width, embed), (width, embed), (width, embed))
    heads = grads(
        head_make, head_shapes, "head_grads", place[:1], seq_count,
        [(o["back"], o["hidden"], cotangent_parts[c]) for c, o in enumerate(stages)],
        small=(small,), after=(last["made"],), times=0,
    )
    merged = elementwise(
        merge_kernel, "merge", [feed, heads[0], partner(heads[1], "seq", 1)],
        (feed.shape[0], feed.shape[1] + heads[0].shape[1], LANES), times=100,
    )
    merged = to_chips(merged, "seq")
    outer_grad, inner_wgrad = unpack(
        place[:1], merged, partner(merged, "seq", 1), feed_shapes, after=tuple(o["both"] for o in stages[:-1])
    )
    heads = elementwise(partial(add_kernel, feed.shape[1]), "add_up", [merged], heads[0].shape)
    heads = to_chips(heads, "seq")

    layer_out, token_grad = last_step(
        [o["both"] for o in outs], [o["stat"] for o in outs], own_tokens, own_cotangent,
        norm_gain.astype(F32)[None], outer_bias.astype(F32)[None], width, shard_len,
    )
    heads = passed_on(heads, (outer_grad, layer_out, token_grad))
    output_grad, query_grad, key_grad, value_grad, *vectors = unpack(
        place[:1], heads, partner(heads, "seq", 1), head_shapes,
        vectors=(local_width, local_width, inner, local_width), small_shape=small_shape,
    )
    gain_grad, shift_grad, inner_bias_grad, outer_bias_grad = (v.reshape(-1) for v in vectors)
    return (
        layer_out, token_grad, gain_grad, shift_grad, query_grad, key_grad, value_grad, output_grad, inner_wgrad,
        inner_bias_grad, outer_grad, outer_bias_grad,
    )


def solution(mesh):
    return jax.shard_map(
        body,
        mesh=mesh,
        in_specs=(
            P("seq", None, "tp"), P("tp"), P("tp"), P(None, "tp"), P(None, "tp"), P(None, "tp"),
            P("tp", None), P(None, "tp"), P("tp"), P("tp", None), P("tp"), P(), P("seq", None, "tp"),
        ),
        out_specs=(
            P("seq", None, "tp"), P("seq", None, "tp"), P("tp"), P("tp"), P(None, "tp"), P(None, "tp"),
            P(None, "tp"), P("tp", None), P(None, "tp"), P("tp"), P("tp", None), P("tp"),
        ),
        check_vma=False,
    )
```

```python
from functools import partial

import jax
import jax.numpy as jnp
from jax import lax
from jax.experimental import pallas as pl
from jax.experimental.pallas import tpu as pltpu
from jax.sharding import PartitionSpec as P

DH = 64
ROTARY = 32
PROTEIN_SLOTS = 8
LANES = 128

EPSILON = 1e-05
SCALING = 0.125
NEGATIVE = -1e30
BASE_FREQ = 10000.0
GELU_A = 0.7978845608028654
GELU_B = 0.044715

F32 = jnp.float32
BF16 = jnp.bfloat16
NT = (((1,), (1,)), ((), ()))
TN = (((0,), (0,)), ((), ()))
VMEM_LIMIT = 56 * 1024 * 1024


def behind(kernel, n_in, after, n_scalar=0):
    n_in = n_in + n_scalar

    def wrapped(*refs):
        return kernel(*refs[:n_in], *refs[n_in + len(after) :])

    return wrapped


def work(flops, bytes_accessed, times=3):
    return pl.CostEstimate(flops=times * flops, bytes_accessed=times * bytes_accessed, transcendentals=0)


def unused(after):
    return [pl.BlockSpec(memory_space=pl.ANY)] * len(after)


def params(**more):
    return pltpu.CompilerParams(vmem_limit_bytes=VMEM_LIMIT, **more)


def packing(lengths, extent):
    protein_ends = jnp.cumsum(lengths, axis=1)
    places = jnp.arange(extent, dtype=jnp.int32)
    passed = protein_ends[:, None, :] <= places[None, :, None]
    begins = jnp.max(jnp.where(passed, protein_ends[:, None, :], 0), axis=2)
    padded = places[None, :] >= protein_ends[:, -1:]
    starts = jnp.where(padded, places[None, :], begins)
    return starts, places[None, :] - starts


def turn_tables(inside_position):
    dim_index = jnp.arange(LANES, dtype=jnp.int32) % DH
    halves = (dim_index // 2).astype(F32)
    frequency = jnp.where(dim_index < ROTARY, BASE_FREQ ** (-2.0 * halves / ROTARY), 0.0)
    sign = jnp.where(dim_index % 2 == 0, -1.0, 1.0)
    phase_angle = inside_position.astype(F32)[..., None] * frequency
    return jnp.cos(phase_angle), jnp.sin(phase_angle) * sign


def swap_pairs(x):
    lane = lax.broadcasted_iota(jnp.int32, x.shape, 1)
    return jnp.where(lane % 2 == 0, pltpu.roll(x, LANES - 1, 1), pltpu.roll(x, 1, 1))


def norm_project_kernel(
    x_ref, gain_ref, shift_ref, wq_ref, wk_ref, wv_ref, win_ref, bias_ref, cos_ref, sin_ref,
    hidden_ref, qkv_ref, act_ref, slope_ref, stat_ref,
):
    parts, rows, part = x_ref.shape
    width = parts * part
    embed = wq_ref.shape[1]
    xs = [x_ref[k].astype(F32) for k in range(parts)]
    mean = sum(jnp.sum(x, axis=1, keepdims=True) for x in xs) * (1.0 / width)
    xs = [x - mean for x in xs]
    var = sum(jnp.sum(x * x, axis=1, keepdims=True) for x in xs) * (1.0 / width)
    inverse = lax.rsqrt(var + EPSILON)
    lane = lax.broadcasted_iota(jnp.int32, stat_ref.shape, 1)
    stat_ref[...] = jnp.where(lane == 0, mean, inverse)
    for k in range(parts):
        at = pl.ds(k * part, part)
        hidden_ref[:, at] = (xs[k] * inverse * gain_ref[:, at] + shift_ref[:, at]).astype(BF16)
    hidden = hidden_ref[...]
    cos, sin = cos_ref[...], sin_ref[...]
    for n, w_ref in enumerate((wq_ref, wk_ref)):
        pre = jnp.dot(hidden, w_ref[...], preferred_element_type=F32)
        for g in range(embed // LANES):
            one = pre[:, g * LANES : (g + 1) * LANES]
            qkv_ref[:, pl.ds(n * embed + g * LANES, LANES)] = (
                one * cos + swap_pairs(one) * sin
            ).astype(BF16)
    qkv_ref[:, pl.ds(2 * embed, embed)] = jnp.dot(
        hidden, wv_ref[...], preferred_element_type=F32
    ).astype(BF16)
    v = jnp.dot(hidden, win_ref[...], preferred_element_type=F32) + bias_ref[...]
    square = v * v
    t = jnp.tanh(GELU_A * v * (1.0 + GELU_B * square))
    act_ref[...] = (0.5 * v * (1.0 + t)).astype(BF16)
    slope_ref[...] = 0.5 * (1.0 + t) + 0.5 * v * (1.0 - t * t) * (
        GELU_A * (1.0 + 3.0 * GELU_B * square)
    )


def norm_project(x, gain, shift, wq, wk, wv, win, bias, cos, sin, after=()):
    parts, total, part = x.shape
    width, embed = wq.shape
    inner = win.shape[1]
    rows = min(256, total)
    whole = lambda i: (0, 0)
    block = lambda i: (i, 0)
    return pl.pallas_call(
        behind(norm_project_kernel, 10, after),
        grid=(total // rows,),
        in_specs=[
            pl.BlockSpec((parts, rows, part), lambda i: (0, i, 0)),
            pl.BlockSpec((1, width), whole),
            pl.BlockSpec((1, width), whole),
            pl.BlockSpec((width, embed), whole),
            pl.BlockSpec((width, embed), whole),
            pl.BlockSpec((width, embed), whole),
            pl.BlockSpec((width, inner), whole),
            pl.BlockSpec((1, inner), whole),
            pl.BlockSpec((rows, LANES), block),
            pl.BlockSpec((rows, LANES), block),
            *unused(after),
        ],
        out_specs=[
            pl.BlockSpec((rows, width), block),
            pl.BlockSpec((rows, 3 * embed), block),
            pl.BlockSpec((rows, inner), block),
            pl.BlockSpec((rows, inner), block),
            pl.BlockSpec((rows, LANES), block),
        ],
        out_shape=[
            jax.ShapeDtypeStruct((total, width), BF16),
            jax.ShapeDtypeStruct((total, 3 * embed), BF16),
            jax.ShapeDtypeStruct((total, inner), BF16),
            jax.ShapeDtypeStruct((total, inner), F32),
            jax.ShapeDtypeStruct((total, LANES), F32),
        ],
        compiler_params=params(),
        cost_estimate=work(2 * total * width * (3 * embed + inner), total * (4 * width + 6 * embed + 6 * inner)),
        name="norm_project",
    )(x, gain, shift, wq, wk, wv, win, bias, cos, sin, *after)


def push_back_kernel(c_ref, wo_ref, wout_ref, slope_ref, mixed_grad_ref, inner_grad_ref, bias_ref):
    parts, rows, part = c_ref.shape
    mixed_grad = inner = None
    for k in range(parts):
        at = pl.ds(k * part, part)
        one = jnp.dot(c_ref[k], wo_ref[at, :], preferred_element_type=F32)
        two = jnp.dot(c_ref[k], wout_ref[at, :], preferred_element_type=F32)
        mixed_grad = one if mixed_grad is None else mixed_grad + one
        inner = two if inner is None else inner + two
    mixed_grad_ref[...] = mixed_grad.astype(BF16)
    inner_low = (inner * slope_ref[...]).astype(BF16)
    inner_grad_ref[...] = inner_low

    @pl.when(pl.program_id(0) == 0)
    def _():
        bias_ref[...] = jnp.zeros_like(bias_ref)

    bias_ref[...] += jnp.sum(inner_low.astype(F32), axis=0, keepdims=True)


def push_back(c, wo, wout, slope, after=(), times=3):
    parts, total, part = c.shape
    width, embed = wo.shape
    inner = wout.shape[1]
    rows = min(512, total)
    whole = lambda i: (0, 0)
    block = lambda i: (i, 0)
    return pl.pallas_call(
        behind(push_back_kernel, 4, after),
        grid=(total // rows,),
        in_specs=[
            pl.BlockSpec((parts, rows, part), lambda i: (0, i, 0)),
            pl.BlockSpec((width, embed), whole),
            pl.BlockSpec((width, inner), whole),
            pl.BlockSpec((rows, inner), block),
            *unused(after),
        ],
        out_specs=[
            pl.BlockSpec((rows, embed), block),
            pl.BlockSpec((rows, inner), block),
            pl.BlockSpec((1, inner), whole),
        ],
        out_shape=[
            jax.ShapeDtypeStruct((total, embed), BF16),
            jax.ShapeDtypeStruct((total, inner), BF16),
            jax.ShapeDtypeStruct((1, inner), F32),
        ],
        compiler_params=params(),
        cost_estimate=work(2 * total * width * (embed + inner), total * (2 * width + 2 * embed + 6 * inner), times),
        name="push_back",
    )(c, wo, wout, slope, *after)


def attend_kernel(
    sizes, variant_ref, q_ref, k_ref, v_ref, g_ref, start_ref, cos_ref, sin_ref, out_ref, dk_ref, dv_ref
):
    at = pl.program_id(0)
    span, embed = q_ref.shape
    groups = [pl.ds(n * LANES, LANES) for n in range(embed // LANES)]
    first = lax.broadcasted_iota(jnp.int32, (span, LANES), 1) < DH
    row_at = pl.multiple_of(at * span, span)

    @pl.when(at == 0)
    def _():
        dk_ref[...] = jnp.zeros_like(dk_ref)
        dv_ref[...] = jnp.zeros_like(dv_ref)

    def unturn(x, cos, sin):
        return x * cos - swap_pairs(x) * sin

    def block(count):
        window = count * span
        base = pl.multiple_of(jnp.maximum(at + 1 - count, 0) * span, span)
        keys_at = pl.ds(base, window)
        rows = pl.ds(row_at, span)
        key_place = base + lax.broadcasted_iota(jnp.int32, (span, window), 1)
        query_place = row_at + lax.broadcasted_iota(jnp.int32, (span, window), 0)
        seen = (key_place >= start_ref[...]) & (key_place <= query_place)
        heads = []
        for group in groups:
            q = q_ref[:, group] * jnp.asarray(SCALING, BF16)
            g = g_ref[:, group]
            for mine in (first, jnp.logical_not(first)):
                heads.append((group, jnp.where(mine, q, jnp.zeros_like(q)), jnp.where(mine, g, jnp.zeros_like(g))))
        scores = [
            lax.dot_general(q, k_ref[keys_at, group], NT, preferred_element_type=F32) for group, q, g in heads
        ]
        pushed = [
            lax.dot_general(g, v_ref[keys_at, group], NT, preferred_element_type=F32) for group, q, g in heads
        ]
        weights = []
        for one in scores:
            one = jnp.where(seen, one, NEGATIVE)
            one = jnp.exp(one - jnp.max(one, axis=1, keepdims=True))
            weights.append(one * (1.0 / jnp.sum(one, axis=1, keepdims=True)))
        lows = [one.astype(BF16) for one in weights]
        grads = [
            (one * (push - jnp.sum(one * push, axis=1, keepdims=True))).astype(BF16)
            for one, push in zip(weights, pushed)
        ]
        for n, group in enumerate(groups):
            keys, values = k_ref[keys_at, group], v_ref[keys_at, group]
            pair = (2 * n, 2 * n + 1)
            mixed = [jnp.dot(lows[h], values, preferred_element_type=F32) for h in pair]
            dq = [jnp.dot(grads[h], keys, preferred_element_type=F32) for h in pair]
            dk_ref[keys_at, group] += sum(tn_dot(grads[h], heads[h][1]) for h in pair)
            dv_ref[keys_at, group] += sum(tn_dot(lows[h], heads[h][2]) for h in pair)
            out_ref[rows, group] = jnp.where(first, mixed[0], mixed[1]).astype(BF16)
            turned = jnp.where(first, dq[0], dq[1]) * SCALING
            out_ref[rows, pl.ds(embed + n * LANES, LANES)] = unturn(
                turned, cos_ref[rows, :], sin_ref[rows, :]
            ).astype(BF16)

    for n, count in enumerate(sizes):

        @pl.when(variant_ref[at] == n)
        def _(count=count):
            block(count)

    @pl.when(at == pl.num_programs(0) - 1)
    def _():
        for n, group in enumerate(groups):
            out_ref[:, pl.ds(2 * embed + n * LANES, LANES)] = unturn(
                dk_ref[:, group], cos_ref[...], sin_ref[...]
            ).astype(BF16)
            out_ref[:, pl.ds(3 * embed + n * LANES, LANES)] = dv_ref[:, group].astype(BF16)


def attend(qkv, g, starts, cos, sin, after=()):
    extent, embed = g.shape
    span = min(256, extent)
    spans = extent // span
    sizes = [size for size in range(1, spans) if size <= 4 or size % 2 == 0] + [spans]
    heads = starts.reshape(spans, span)[:, 0]
    need = jnp.arange(spans, dtype=jnp.int32) - heads // span + 1
    variant = jnp.sum((need[:, None] > jnp.asarray(sizes, jnp.int32)[None, :]).astype(jnp.int32), axis=1)
    spec = pl.BlockSpec
    return pl.pallas_call(
        behind(partial(attend_kernel, tuple(sizes)), 7, after, 1),
        grid_spec=pltpu.PrefetchScalarGridSpec(
            num_scalar_prefetch=1,
            grid=(spans,),
            in_specs=[
                spec((span, embed), lambda i, s: (i, 0)),
                spec((extent, embed), lambda i, s: (0, 1)),
                spec((extent, embed), lambda i, s: (0, 2)),
                spec((span, embed), lambda i, s: (i, 0)),
                spec((span, 1), lambda i, s: (i, 0)),
                spec((extent, LANES), lambda i, s: (0, 0)),
                spec((extent, LANES), lambda i, s: (0, 0)),
                *unused(after),
            ],
            out_specs=spec((extent, 4 * embed), lambda i, s: (0, 0)),
            scratch_shapes=[pltpu.VMEM((extent, embed), F32), pltpu.VMEM((extent, embed), F32)],
        ),
        out_shape=jax.ShapeDtypeStruct((extent, 4 * embed), BF16),
        compiler_params=params(),
        cost_estimate=work(12 * embed * extent * extent, extent * embed * 16),
        name="attend",
    )(variant, qkv, qkv, qkv, g, starts[:, None], cos, sin, *after)


def dense_back_kernel(
    back_ref, inner_ref, act_ref, x_ref, stat_ref, gain_ref, wqkv_ref, win_ref, wo_ref, wout_ref,
    out_ref, feature_ref, sums_ref,
):
    parts, rows, part = x_ref.shape
    extra = sums_ref.shape[0]
    total_rows = (out_ref.shape[1] - extra) // 2
    embed = wo_ref.shape[0]
    step = pl.program_id(0)
    mean, inverse = stat_ref[:, 0:1], stat_ref[:, 1:2]

    @pl.when(step == 0)
    def _():
        feature_ref[...] = jnp.zeros_like(feature_ref)
        sums_ref[...] = jnp.zeros_like(sums_ref)

    first = pl.ds(pl.multiple_of(step * rows, rows), rows)
    second = pl.ds(pl.multiple_of(total_rows + step * rows, rows), rows)
    ones = jnp.ones((8, LANES), BF16)
    one = two = None
    for k in range(parts):
        at = pl.ds(k * part, part)
        total = jnp.dot(inner_ref[...], win_ref[:, at], preferred_element_type=F32)
        total += jnp.dot(
            back_ref[:, pl.ds(embed, 3 * embed)], wqkv_ref[:, at], preferred_element_type=F32
        )
        out_ref[k, first, :] = total.astype(BF16)
        out_ref[k, second, :] = (
            jnp.dot(back_ref[:, pl.ds(0, embed)], wo_ref[:, at], preferred_element_type=F32)
            + jnp.dot(act_ref[...], wout_ref[:, at], preferred_element_type=F32)
        ).astype(BF16)
        scaled = (x_ref[k].astype(F32) - mean) * inverse
        product = total * scaled
        feature_ref[0:1, at] += jnp.sum(product, axis=0, keepdims=True)
        feature_ref[1:2, at] += jnp.sum(total, axis=0, keepdims=True)
        gain = gain_ref[:, at]
        for n in range(part // LANES):
            lanes = slice(n * LANES, (n + 1) * LANES)
            gained, moved = total[:, lanes] * gain[:, lanes], product[:, lanes] * gain[:, lanes]
            one = gained if one is None else one + gained
            two = moved if two is None else two + moved
    one, two = (
        lax.dot_general(ones, sums.astype(BF16), NT, preferred_element_type=F32) for sums in (one, two)
    )
    pieces = max(rows // part, 1)
    for start, row in ((0, one), (total_rows // part, two)):
        for n in range(pieces):
            sums_ref[pl.ds(start + step * pieces + n, 1), :] = row[0:1, n * part : (n + 1) * part]

    @pl.when(step == pl.num_programs(0) - 1)
    def _():
        for k in range(parts):
            out_ref[k, pl.ds(2 * total_rows, extra), :] = sums_ref[...].astype(BF16)


def extra_rows(total, part):
    return -(-2 * total // part // 16) * 16


def dense_back(back, inner_grad, act, x, stat, gain, wqkv, win, wo, wout, after=()):
    parts, total, part = x.shape
    embed, width = wo.shape
    inner = win.shape[0]
    rows = min(512, total)
    extra = extra_rows(total, part)
    whole = lambda i: (0, 0)
    block = lambda i: (i, 0)
    return pl.pallas_call(
        behind(dense_back_kernel, 10, after),
        grid=(total // rows,),
        in_specs=[
            pl.BlockSpec((rows, 4 * embed), block),
            pl.BlockSpec((rows, inner), block),
            pl.BlockSpec((rows, inner), block),
            pl.BlockSpec((parts, rows, part), lambda i: (0, i, 0)),
            pl.BlockSpec((rows, LANES), block),
            pl.BlockSpec((1, width), whole),
            pl.BlockSpec((3 * embed, width), whole),
            pl.BlockSpec((inner, width), whole),
            pl.BlockSpec((embed, width), whole),
            pl.BlockSpec((inner, width), whole),
            *unused(after),
        ],
        out_specs=[
            pl.BlockSpec((parts, 2 * total + extra, part), lambda i: (0, 0, 0)),
            pl.BlockSpec((2, width), whole),
        ],
        out_shape=[
            jax.ShapeDtypeStruct((parts, 2 * total + extra, part), BF16),
            jax.ShapeDtypeStruct((2, width), F32),
        ],
        scratch_shapes=[pltpu.VMEM((extra, part), F32)],
        compiler_params=params(),
        cost_estimate=work(2 * total * width * (4 * embed + 2 * inner), total * (6 * width + 8 * embed + 4 * inner)),
        name="dense_back",
    )(back, inner_grad, act, x, stat, gain, wqkv, win, wo, wout, *after)


def tn_dot(left, right):
    return lax.dot_general(left, right, TN, preferred_element_type=F32)


def piece_rows(shapes, devices):
    return [rows * columns // (devices * LANES) for rows, columns in shapes]


def grads_kernel(chunks, steps, n_in, n_small, make, core_ref, *refs):
    at = chunks * n_in
    ins, small_refs, refs = refs[:at], refs[at : at + n_small], refs[at + n_small :]
    keep_ref, send_ref, *totals = refs
    at = pl.program_id(0)

    @pl.when(at == 0)
    def _():
        for total in totals:
            total[...] = jnp.zeros_like(total)

    for c in range(chunks):

        @pl.when(at // steps == c)
        def _(c=c):
            make(ins[c * n_in : (c + 1) * n_in], totals)

    @pl.when(at == chunks * steps - 1)
    def _():
        chips = keep_ref.shape[0]
        for core, out_ref in ((core_ref[0], keep_ref), (1 - core_ref[0], send_ref)):
            for chip in range(chips):
                offset = 0
                for total in (*totals, *small_refs):
                    rows = total.shape[0] // (2 * chips)
                    start = pl.multiple_of((core * chips + chip) * rows, rows)
                    for n in range(total.shape[1] // LANES):
                        out_ref[chip, pl.ds(offset, rows), :] = total[
                            pl.ds(start, rows), pl.ds(n * LANES, LANES)
                        ].astype(BF16)
                        offset += rows


def feed_make(ins, totals):
    act, hidden, inner_grad, cot = ins
    outer_total, inner_total = totals
    parts, _, part = cot.shape
    left = act[...]
    for k in range(parts):
        outer_total[:, pl.ds(k * part, part)] += tn_dot(left, cot[k])
    inner_total[...] += tn_dot(hidden[...], inner_grad[...])


def head_make(ins, totals):
    back, hidden, cot = ins
    output_total, *projection_totals = totals
    parts, _, part = cot.shape
    embed = output_total.shape[0]
    left = back[:, pl.ds(0, embed)]
    for k in range(parts):
        output_total[:, pl.ds(k * part, part)] += tn_dot(left, cot[k])
    for n, total in enumerate(projection_totals):
        total[...] += tn_dot(hidden[...], back[:, pl.ds((n + 1) * embed, embed)])


def grads(make, shapes, name, core, devices, chunk_arrays, small=(), after=(), times=3):
    chunks = len(chunk_arrays)
    total = chunk_arrays[0][0].shape[0]
    rows = min(512, total)
    steps = total // rows
    specs, arrays = [], []
    for c, group in enumerate(chunk_arrays):
        pick = lambda i, c=c: jnp.clip(i - c * steps, 0, steps - 1)
        for array in group:
            if array.ndim == 2:
                specs.append(pl.BlockSpec((rows, array.shape[1]), lambda i, s, pick=pick: (pick(i), 0)))
            else:
                specs.append(
                    pl.BlockSpec((array.shape[0], rows, array.shape[2]), lambda i, s, pick=pick: (0, pick(i), 0))
                )
            arrays.append(array)
    for array in small:
        specs.append(pl.BlockSpec(array.shape, lambda i, s: (0, 0)))
        arrays.append(array)
    packed = (devices // 2, sum(piece_rows((*shapes, *[a.shape for a in small]), devices)), LANES)
    kernel = partial(grads_kernel, chunks, steps, len(chunk_arrays[0]), len(small), make)
    return pl.pallas_call(
        behind(kernel, len(specs), after, 1),
        grid_spec=pltpu.PrefetchScalarGridSpec(
            num_scalar_prefetch=1,
            grid=(chunks * steps,),
            in_specs=specs + unused(after),
            out_specs=[pl.BlockSpec(packed, lambda i, s: (0, 0, 0))] * 2,
            scratch_shapes=[pltpu.VMEM(shape, F32) for shape in shapes],
        ),
        out_shape=[jax.ShapeDtypeStruct(packed, BF16)] * 2,
        compiler_params=params(),
        cost_estimate=work(
            sum(2 * chunks * total * a * b for a, b in shapes), 2 * sum(a.size for a in arrays), times
        ),
        name=name,
    )(core, *arrays, *after)


def fold_kernel(*refs):
    for n in range(refs[-1].shape[0]):
        refs[-1][n] = sum(ref[n].astype(F32) for ref in refs[:-1]).astype(BF16)


def elementwise(kernel, name, arrays, shape=None, after=()):
    spec = pl.BlockSpec(memory_space=pltpu.VMEM)
    shape = arrays[0].shape if shape is None else shape
    return pl.pallas_call(
        behind(kernel, len(arrays), after),
        in_specs=[spec] * len(arrays) + unused(after),
        out_specs=spec,
        out_shape=jax.ShapeDtypeStruct(shape, BF16),
        compiler_params=params(),
        cost_estimate=work(3 * arrays[0].size, 6 * arrays[0].size),
        name=name,
    )(*arrays, *after)


def merge_kernel(pieces_ref, keep_ref, came_ref, out_ref):
    rows = pieces_ref.shape[1]
    total = pieces_ref[0].astype(F32)
    for n in range(1, pieces_ref.shape[0]):
        total += pieces_ref[n].astype(F32)
    total = total.astype(BF16)
    for n in range(out_ref.shape[0]):
        out_ref[n, pl.ds(0, rows), :] = total
        out_ref[n, pl.ds(rows, keep_ref.shape[1]), :] = (
            keep_ref[n].astype(F32) + came_ref[n].astype(F32)
        ).astype(BF16)


def add_kernel(skip, x_ref, out_ref):
    rows = pl.ds(skip, out_ref.shape[1])
    total = x_ref[0, rows, :].astype(F32)
    for n in range(1, x_ref.shape[0]):
        total += x_ref[n, rows, :].astype(F32)
    total = total.astype(BF16)
    for n in range(out_ref.shape[0]):
        out_ref[n] = total


def passed_on(array, after):
    spec = pl.BlockSpec(memory_space=pl.ANY)
    return pl.pallas_call(
        lambda *refs: None,
        in_specs=[spec] * (1 + len(after)),
        out_specs=spec,
        out_shape=jax.ShapeDtypeStruct(array.shape, array.dtype),
        input_output_aliases={0: 0},
        compiler_params=params(),
        name="passed_on",
    )(array, *after)


def unpack_kernel(n_out, core_ref, own_ref, other_ref, *refs):
    matrix_refs, vector_refs, small_refs = refs[:n_out], refs[n_out:], ()
    if len(refs) > n_out:
        vector_refs, small_refs = refs[n_out:-1], refs[-1:]
    chips = own_ref.shape[0]
    for core, ref in ((core_ref[0], own_ref), (1 - core_ref[0], other_ref)):
        for chip in range(chips):
            offset = 0
            for out_ref in (*matrix_refs, *small_refs):
                rows = out_ref.shape[0] // (2 * chips)
                start = pl.multiple_of((core * chips + chip) * rows, rows)
                for block in range(out_ref.shape[1] // LANES):
                    out_ref[pl.ds(start, rows), pl.ds(block * LANES, LANES)] = ref[
                        chip, pl.ds(offset, rows), :
                    ].astype(F32)
                    offset += rows
    row = 0
    for out_ref in vector_refs:
        for block in range(out_ref.shape[1] // LANES):
            out_ref[:, pl.ds(block * LANES, LANES)] = small_refs[0][pl.ds(row, 1), :]
            row += 1


def unpack(core, own, other, shapes, vectors=(), small_shape=None, after=()):
    spec = pl.BlockSpec(memory_space=pltpu.VMEM)
    outs = (*shapes, *[(1, size) for size in vectors])
    return pl.pallas_call(
        behind(partial(unpack_kernel, len(shapes)), 2, after, 1),
        in_specs=[pl.BlockSpec(memory_space=pltpu.SMEM), spec, spec] + unused(after),
        out_specs=[spec] * len(outs),
        out_shape=[jax.ShapeDtypeStruct(shape, F32) for shape in outs],
        scratch_shapes=[pltpu.VMEM(small_shape, F32)] if vectors else [],
        compiler_params=params(),
        cost_estimate=work(own.size, 12 * own.size),
        name="unpack",
    )(core, own, other, *after)


def last_step_kernel(chunks, width, *refs):
    both_refs, stat_refs, tok_refs, cot_refs = (refs[n * chunks : (n + 1) * chunks] for n in range(4))
    gain_ref, bias_ref, out_ref, grad_ref, plain_ref, columns_ref = refs[4 * chunks :]
    per, span, part = tok_refs[0].shape
    halves = part // LANES
    total = per * LANES
    step = pl.program_id(0)

    @pl.when(step == 0)
    def _():
        for c, both_ref in enumerate(both_refs):
            sums = both_ref[pl.ds(2 * total, both_ref.shape[0] - 2 * total), :]
            shape = (sums.shape[0], LANES)
            eye = lax.broadcasted_iota(jnp.int32, shape, 0) == lax.broadcasted_iota(jnp.int32, shape, 1)
            for h in range(halves):
                columns_ref[c * halves + h] = tn_dot(
                    sums[:, h * LANES : (h + 1) * LANES], eye.astype(F32).astype(BF16)
                ) * (1.0 / width)

    here = pl.ds(pl.multiple_of(step * span, span), span)
    for c, (both_ref, stat_ref, tok_ref, cot_ref) in enumerate(zip(both_refs, stat_refs, tok_refs, cot_refs)):
        for n in range(per):
            r = c * per + n
            at = n * LANES + step * span
            hidden_grad = both_ref[pl.ds(pl.multiple_of(at, span), span), :].astype(F32)
            branch = both_ref[pl.ds(pl.multiple_of(total + at, span), span), :].astype(F32)
            columns = columns_ref[c * halves + n % halves, here, :]
            first = columns[:, n // halves : n // halves + 1]
            second = columns[:, (per + n) // halves : (per + n) // halves + 1]
            mean, inverse = stat_ref[n, :, 0:1], stat_ref[n, :, 1:2]
            token = tok_ref[n].astype(F32)
            scaled = (token - mean) * inverse
            plain_ref[:, r, :] = token + branch + bias_ref[...]
            grad_ref[:, r, :] = cot_ref[n].astype(F32) + inverse * (
                hidden_grad * gain_ref[...] - first - scaled * second
            )
    out_ref[...] = plain_ref[...].astype(BF16)


def last_step(boths, stats, tokens, cotangents, gain, bias, width, positions):
    chunks = len(boths)
    total, part = tokens[0].shape
    per = total // positions
    rows = chunks * per
    in_rows = lambda array: array.reshape(per, positions, array.shape[1])
    span = min(32, positions)
    return pl.pallas_call(
        partial(last_step_kernel, chunks, width),
        grid=(positions // span,),
        in_specs=[
            *[pl.BlockSpec(both.shape, lambda i: (0, 0)) for both in boths],
            *[pl.BlockSpec((per, span, LANES), lambda i: (0, i, 0))] * chunks,
            *[pl.BlockSpec((per, span, part), lambda i: (0, i, 0))] * (2 * chunks),
            *[pl.BlockSpec((1, part), lambda i: (0, 0))] * 2,
        ],
        out_specs=[pl.BlockSpec((span, rows, part), lambda i: (i, 0, 0))] * 2,
        out_shape=[
            jax.ShapeDtypeStruct((positions, rows, part), BF16),
            jax.ShapeDtypeStruct((positions, rows, part), F32),
        ],
        scratch_shapes=[
            pltpu.VMEM((span, rows, part), F32),
            pltpu.VMEM((chunks * (part // LANES), LANES, LANES), F32),
        ],
        compiler_params=params(),
        cost_estimate=work(20 * total * part, 12 * total * part),
        name="last_step",
    )(*boths, *map(in_rows, (*stats, *tokens, *cotangents)), gain, bias)


def partner(array, axis, bit):
    size = lax.axis_size(axis)
    return lax.ppermute(array, axis, [(i, i ^ bit) for i in range(size)])


def to_chips(pieces, axis):
    size = lax.axis_size(axis)
    groups = [list(range(core, size, 2)) for core in range(2)]
    return lax.all_to_all(pieces, axis, 0, 0, tiled=True, axis_index_groups=groups)


def small_sum(array, axes):
    for axis in axes:
        bit = 1
        while bit < lax.axis_size(axis):
            array = array + partner(array, axis, bit)
            bit *= 2
    return array


def body(
    tokens, norm_gain, norm_shift, query_weight, key_weight, value_weight, output_weight,
    inner_weight, inner_bias, outer_weight, outer_bias, lengths, cotangent,
):
    shard_len, batch_rows, local_width = tokens.shape
    seq_count, tp_count = lax.axis_size("seq"), lax.axis_size("tp")
    position, width_index = lax.axis_index("seq"), lax.axis_index("tp")
    extent = shard_len * seq_count
    width, embed = query_weight.shape
    inner = inner_weight.shape[1]
    chunks = batch_rows // seq_count

    own_tokens, own_cotangent = (
        [part.reshape(extent, local_width) for part in jnp.split(jnp.swapaxes(array, 0, 1), chunks)]
        for array in (tokens, cotangent)
    )
    back_qkv = jnp.concatenate([w.T for w in (query_weight, key_weight, value_weight)], axis=0)
    back_inner, back_output, back_outer = inner_weight.T, output_weight.T, outer_weight.T
    token_parts = [lax.all_gather(own_tokens[c], "tp") for c in range(chunks)]
    cotangent_parts = [lax.all_gather(own_cotangent[c], "tp") for c in range(chunks)]
    vectors = lax.all_gather(jnp.stack([norm_gain, norm_shift]), "tp", axis=1, tiled=True)
    vectors = vectors.astype(F32)
    gain, shift = vectors[0:1], vectors[1:2]

    starts, places = packing(lengths, extent)
    own_places = lax.dynamic_slice_in_dim(places, position * shard_len, shard_len, 1)
    own_cos, own_sin = turn_tables(own_places.reshape(chunks, extent))
    row_starts = [lax.dynamic_index_in_dim(starts, c * seq_count + position, 0, False) for c in range(chunks)]
    row_places = [lax.dynamic_index_in_dim(places, c * seq_count + position, 0, False) for c in range(chunks)]
    row_tables = [turn_tables(row) for row in row_places]
    bias_row = inner_bias.astype(F32)[None]

    def exchange(array):
        split = array.reshape(seq_count, shard_len, array.shape[-1])
        return lax.all_to_all(split, "seq", 0, 0, tiled=True).reshape(extent, array.shape[-1])

    stages = [dict() for _ in range(chunks)]
    place = jnp.stack([position % 2, position // 2]).astype(jnp.int32)
    feed_shapes = ((inner, width), (width, inner))

    def project(c, after=()):
        o = stages[c]
        o["hidden"], qkv, o["act"], o["slope"], o["stat"] = norm_project(
            token_parts[c], gain, shift, query_weight, key_weight, value_weight, inner_weight,
            bias_row, own_cos[c], own_sin[c], after=after,
        )
        o["qkv_rows"] = exchange(qkv)

    def push(c, after=()):
        o = stages[c]
        mixed_grad, o["inner_grad"], o["bias"] = push_back(
            cotangent_parts[c], back_output, back_outer, o["slope"], after=after, times=20 if c else 3
        )
        o["grad_rows"] = exchange(mixed_grad)

    def feed_grads(c):
        o = stages[c]
        keep, send = grads(
            feed_make, feed_shapes, "feed_grads", place[:1], seq_count,
            [(o["act"], o["hidden"], o["inner_grad"], cotangent_parts[c])],
        )
        return keep, partner(send, "seq", 1)

    def mix(c, after=()):
        o = stages[c]
        o["attention"] = attend(o["qkv_rows"], o["grad_rows"], row_starts[c], *row_tables[c], after=after)
        o["back"] = exchange(o["attention"])

    def finish(c, after=()):
        o = stages[c]
        o["made"], o["feature"] = dense_back(
            o["back"], o["inner_grad"], o["act"], token_parts[c], o["stat"], gain, back_qkv, back_inner,
            output_weight, outer_weight, after=after,
        )
        o["both"] = lax.psum_scatter(o["made"], "tp", scatter_dimension=0)

    feed = []
    for c in range(chunks):
        if c == 0:
            project(c)
            push(c, after=(stages[c]["qkv_rows"], back_qkv, back_inner))
        else:
            project(c, after=(stages[c - 1]["attention"],))
            finish(c - 1, after=(stages[c]["hidden"],))
            push(c, after=(stages[c - 1]["made"], stages[c]["qkv_rows"]))
        feed.extend(feed_grads(c))
        mix(c, after=(feed[-2],))
    outs = stages

    def both(make):
        return sum(make(c, outs[c]) for c in range(chunks))

    last = stages[-1]
    feed = elementwise(fold_kernel, "fold", feed, after=(last["attention"],))
    finish(chunks - 1, after=(feed,))
    feed = to_chips(feed, "seq")

    feature = small_sum(both(lambda c, o: o["feature"]).reshape(-1, LANES), ("tp",)).reshape(2, width)
    feature = lax.dynamic_slice_in_dim(feature, width_index * local_width, local_width, 1)
    small = jnp.concatenate(
        [
            feature.reshape(-1), both(lambda c, o: o["bias"])[0],
            jnp.sum(cotangent.astype(F32), axis=(0, 1)),
        ]
    )
    small_shape = (seq_count * 16, LANES)
    small = jnp.pad(small, (0, small_shape[0] * LANES - small.size)).reshape(small_shape)
    head_shapes = ((embed, width), (width, embed), (width, embed), (width, embed))
    heads = grads(
        head_make, head_shapes, "head_grads", place[:1], seq_count,
        [(o["back"], o["hidden"], cotangent_parts[c]) for c, o in enumerate(stages)],
        small=(small,), after=(last["made"],), times=0,
    )
    merged = elementwise(
        merge_kernel, "merge", [feed, heads[0], partner(heads[1], "seq", 1)],
        (feed.shape[0], feed.shape[1] + heads[0].shape[1], LANES),
    )
    merged = to_chips(merged, "seq")
    outer_grad, inner_wgrad = unpack(
        place[:1], merged, partner(merged, "seq", 1), feed_shapes, after=tuple(o["both"] for o in stages[:-1])
    )
    heads = elementwise(partial(add_kernel, feed.shape[1]), "add_up", [merged], heads[0].shape)
    heads = to_chips(heads, "seq")

    layer_out, token_grad = last_step(
        [o["both"] for o in outs], [o["stat"] for o in outs], own_tokens, own_cotangent,
        norm_gain.astype(F32)[None], outer_bias.astype(F32)[None], width, shard_len,
    )
    heads = passed_on(heads, (outer_grad, layer_out, token_grad))
    output_grad, query_grad, key_grad, value_grad, *vectors = unpack(
        place[:1], heads, partner(heads, "seq", 1), head_shapes,
        vectors=(local_width, local_width, inner, local_width), small_shape=small_shape,
    )
    gain_grad, shift_grad, inner_bias_grad, outer_bias_grad = (v.reshape(-1) for v in vectors)
    return (
        layer_out, token_grad, gain_grad, shift_grad, query_grad, key_grad, value_grad, output_grad, inner_wgrad,
        inner_bias_grad, outer_grad, outer_bias_grad,
    )


def solution(mesh):
    return jax.shard_map(
        body,
        mesh=mesh,
        in_specs=(
            P("seq", None, "tp"), P("tp"), P("tp"), P(None, "tp"), P(None, "tp"), P(None, "tp"),
            P("tp", None), P(None, "tp"), P("tp"), P("tp", None), P("tp"), P(), P("seq", None, "tp"),
        ),
        out_specs=(
            P("seq", None, "tp"), P("seq", None, "tp"), P("tp"), P("tp"), P(None, "tp"), P(None, "tp"),
            P(None, "tp"), P("tp", None), P(None, "tp"), P("tp"), P("tp", None), P("tp"),
        ),
        check_vma=False,
    )
```

```python
from functools import partial

import jax
import jax.numpy as jnp
from jax import lax
from jax.experimental import pallas as pl
from jax.experimental.pallas import tpu as pltpu
from jax.sharding import PartitionSpec as P

DH = 64
ROTARY = 32
PROTEIN_SLOTS = 8
LANES = 128

EPSILON = 1e-05
SCALING = 0.125
NEGATIVE = -1e30
BASE_FREQ = 10000.0
GELU_A = 0.7978845608028654
GELU_B = 0.044715

F32 = jnp.float32
BF16 = jnp.bfloat16
NT = (((1,), (1,)), ((), ()))
TN = (((0,), (0,)), ((), ()))
VMEM_LIMIT = 56 * 1024 * 1024


def behind(kernel, n_in, after, n_scalar=0):
    n_in = n_in + n_scalar

    def wrapped(*refs):
        return kernel(*refs[:n_in], *refs[n_in + len(after) :])

    return wrapped


def work(flops, bytes_accessed, times=3):
    return pl.CostEstimate(flops=times * flops, bytes_accessed=times * bytes_accessed, transcendentals=0)


def unused(after):
    return [pl.BlockSpec(memory_space=pl.ANY)] * len(after)


def params(**more):
    return pltpu.CompilerParams(vmem_limit_bytes=VMEM_LIMIT, **more)


def packing(lengths, extent):
    protein_ends = jnp.cumsum(lengths, axis=1)
    places = jnp.arange(extent, dtype=jnp.int32)
    passed = protein_ends[:, None, :] <= places[None, :, None]
    begins = jnp.max(jnp.where(passed, protein_ends[:, None, :], 0), axis=2)
    padded = places[None, :] >= protein_ends[:, -1:]
    starts = jnp.where(padded, places[None, :], begins)
    return starts, places[None, :] - starts


def turn_tables(inside_position):
    dim_index = jnp.arange(LANES, dtype=jnp.int32) % DH
    halves = (dim_index // 2).astype(F32)
    frequency = jnp.where(dim_index < ROTARY, BASE_FREQ ** (-2.0 * halves / ROTARY), 0.0)
    sign = jnp.where(dim_index % 2 == 0, -1.0, 1.0)
    phase_angle = inside_position.astype(F32)[..., None] * frequency
    return jnp.cos(phase_angle), jnp.sin(phase_angle) * sign


def swap_pairs(x):
    lane = lax.broadcasted_iota(jnp.int32, x.shape, 1)
    return jnp.where(lane % 2 == 0, pltpu.roll(x, LANES - 1, 1), pltpu.roll(x, 1, 1))


def norm_project_kernel(
    x_ref, gain_ref, shift_ref, wq_ref, wk_ref, wv_ref, win_ref, bias_ref, wout_ref, cos_ref, sin_ref,
    hidden_ref, qkv_ref, act_ref, slope_ref, stat_ref, branch_ref,
):
    parts, rows, part = x_ref.shape
    width = parts * part
    embed = wq_ref.shape[1]
    xs = [x_ref[k].astype(F32) for k in range(parts)]
    mean = sum(jnp.sum(x, axis=1, keepdims=True) for x in xs) * (1.0 / width)
    xs = [x - mean for x in xs]
    var = sum(jnp.sum(x * x, axis=1, keepdims=True) for x in xs) * (1.0 / width)
    inverse = lax.rsqrt(var + EPSILON)
    lane = lax.broadcasted_iota(jnp.int32, stat_ref.shape, 1)
    stat_ref[...] = jnp.where(lane == 0, mean, inverse)
    for k in range(parts):
        at = pl.ds(k * part, part)
        hidden_ref[:, at] = (xs[k] * inverse * gain_ref[:, at] + shift_ref[:, at]).astype(BF16)
    hidden = hidden_ref[...]
    cos, sin = cos_ref[...], sin_ref[...]
    for n, w_ref in enumerate((wq_ref, wk_ref)):
        pre = jnp.dot(hidden, w_ref[...], preferred_element_type=F32)
        for g in range(embed // LANES):
            one = pre[:, g * LANES : (g + 1) * LANES]
            qkv_ref[:, pl.ds(n * embed + g * LANES, LANES)] = (
                one * cos + swap_pairs(one) * sin
            ).astype(BF16)
    qkv_ref[:, pl.ds(2 * embed, embed)] = jnp.dot(
        hidden, wv_ref[...], preferred_element_type=F32
    ).astype(BF16)
    v = jnp.dot(hidden, win_ref[...], preferred_element_type=F32) + bias_ref[...]
    square = v * v
    t = jnp.tanh(GELU_A * v * (1.0 + GELU_B * square))
    act_ref[...] = (0.5 * v * (1.0 + t)).astype(BF16)
    slope_ref[...] = 0.5 * (1.0 + t) + 0.5 * v * (1.0 - t * t) * (
        GELU_A * (1.0 + 3.0 * GELU_B * square)
    )
    branch_ref[...] = jnp.dot(act_ref[...], wout_ref[...], preferred_element_type=F32).astype(BF16)


def norm_project(x, gain, shift, wq, wk, wv, win, bias, wout, cos, sin, after=()):
    parts, total, part = x.shape
    width, embed = wq.shape
    inner = win.shape[1]
    rows = min(256, total)
    whole = lambda i: (0, 0)
    block = lambda i: (i, 0)
    return pl.pallas_call(
        behind(norm_project_kernel, 11, after),
        grid=(total // rows,),
        in_specs=[
            pl.BlockSpec((parts, rows, part), lambda i: (0, i, 0)),
            pl.BlockSpec((1, width), whole),
            pl.BlockSpec((1, width), whole),
            pl.BlockSpec((width, embed), whole),
            pl.BlockSpec((width, embed), whole),
            pl.BlockSpec((width, embed), whole),
            pl.BlockSpec((width, inner), whole),
            pl.BlockSpec((1, inner), whole),
            pl.BlockSpec((inner, width), whole),
            pl.BlockSpec((rows, LANES), block),
            pl.BlockSpec((rows, LANES), block),
            *unused(after),
        ],
        out_specs=[
            pl.BlockSpec((rows, width), block),
            pl.BlockSpec((rows, 3 * embed), block),
            pl.BlockSpec((rows, inner), block),
            pl.BlockSpec((rows, inner), block),
            pl.BlockSpec((rows, LANES), block),
            pl.BlockSpec((rows, width), block),
        ],
        out_shape=[
            jax.ShapeDtypeStruct((total, width), BF16),
            jax.ShapeDtypeStruct((total, 3 * embed), BF16),
            jax.ShapeDtypeStruct((total, inner), BF16),
            jax.ShapeDtypeStruct((total, inner), F32),
            jax.ShapeDtypeStruct((total, LANES), F32),
            jax.ShapeDtypeStruct((total, width), BF16),
        ],
        compiler_params=params(),
        cost_estimate=work(2 * total * width * (3 * embed + inner), total * (4 * width + 6 * embed + 6 * inner)),
        name="norm_project",
    )(x, gain, shift, wq, wk, wv, win, bias, wout, cos, sin, *after)


def push_back_kernel(c_ref, wo_ref, wout_ref, slope_ref, mixed_grad_ref, inner_grad_ref, bias_ref):
    parts, rows, part = c_ref.shape
    mixed_grad = inner = None
    for k in range(parts):
        at = pl.ds(k * part, part)
        one = jnp.dot(c_ref[k], wo_ref[at, :], preferred_element_type=F32)
        two = jnp.dot(c_ref[k], wout_ref[at, :], preferred_element_type=F32)
        mixed_grad = one if mixed_grad is None else mixed_grad + one
        inner = two if inner is None else inner + two
    mixed_grad_ref[...] = mixed_grad.astype(BF16)
    inner_low = (inner * slope_ref[...]).astype(BF16)
    inner_grad_ref[...] = inner_low

    @pl.when(pl.program_id(0) == 0)
    def _():
        bias_ref[...] = jnp.zeros_like(bias_ref)

    bias_ref[...] += jnp.sum(inner_low.astype(F32), axis=0, keepdims=True)


def push_back(c, wo, wout, slope, after=(), times=3):
    parts, total, part = c.shape
    width, embed = wo.shape
    inner = wout.shape[1]
    rows = min(512, total)
    whole = lambda i: (0, 0)
    block = lambda i: (i, 0)
    return pl.pallas_call(
        behind(push_back_kernel, 4, after),
        grid=(total // rows,),
        in_specs=[
            pl.BlockSpec((parts, rows, part), lambda i: (0, i, 0)),
            pl.BlockSpec((width, embed), whole),
            pl.BlockSpec((width, inner), whole),
            pl.BlockSpec((rows, inner), block),
            *unused(after),
        ],
        out_specs=[
            pl.BlockSpec((rows, embed), block),
            pl.BlockSpec((rows, inner), block),
            pl.BlockSpec((1, inner), whole),
        ],
        out_shape=[
            jax.ShapeDtypeStruct((total, embed), BF16),
            jax.ShapeDtypeStruct((total, inner), BF16),
            jax.ShapeDtypeStruct((1, inner), F32),
        ],
        compiler_params=params(),
        cost_estimate=work(2 * total * width * (embed + inner), total * (2 * width + 2 * embed + 6 * inner), times),
        name="push_back",
    )(c, wo, wout, slope, *after)


def attend_kernel(
    sizes, variant_ref, q_ref, k_ref, v_ref, g_ref, start_ref, cos_ref, sin_ref, out_ref, dk_ref, dv_ref
):
    at = pl.program_id(0)
    span, embed = q_ref.shape
    groups = [pl.ds(n * LANES, LANES) for n in range(embed // LANES)]
    first = lax.broadcasted_iota(jnp.int32, (span, LANES), 1) < DH
    row_at = pl.multiple_of(at * span, span)

    @pl.when(at == 0)
    def _():
        dk_ref[...] = jnp.zeros_like(dk_ref)
        dv_ref[...] = jnp.zeros_like(dv_ref)

    def unturn(x, cos, sin):
        return x * cos - swap_pairs(x) * sin

    def block(count):
        window = count * span
        base = pl.multiple_of(jnp.maximum(at + 1 - count, 0) * span, span)
        keys_at = pl.ds(base, window)
        rows = pl.ds(row_at, span)
        key_place = base + lax.broadcasted_iota(jnp.int32, (span, window), 1)
        query_place = row_at + lax.broadcasted_iota(jnp.int32, (span, window), 0)
        seen = (key_place >= start_ref[...]) & (key_place <= query_place)
        heads = []
        for group in groups:
            q = q_ref[:, group] * jnp.asarray(SCALING, BF16)
            g = g_ref[:, group]
            for mine in (first, jnp.logical_not(first)):
                heads.append((group, jnp.where(mine, q, jnp.zeros_like(q)), jnp.where(mine, g, jnp.zeros_like(g))))
        scores = [
            lax.dot_general(q, k_ref[keys_at, group], NT, preferred_element_type=F32) for group, q, g in heads
        ]
        pushed = [
            lax.dot_general(g, v_ref[keys_at, group], NT, preferred_element_type=F32) for group, q, g in heads
        ]
        weights = []
        for one in scores:
            one = jnp.where(seen, one, NEGATIVE)
            one = jnp.exp(one - jnp.max(one, axis=1, keepdims=True))
            weights.append(one * (1.0 / jnp.sum(one, axis=1, keepdims=True)))
        lows = [one.astype(BF16) for one in weights]
        grads = [
            (one * (push - jnp.sum(one * push, axis=1, keepdims=True))).astype(BF16)
            for one, push in zip(weights, pushed)
        ]
        for n, group in enumerate(groups):
            keys, values = k_ref[keys_at, group], v_ref[keys_at, group]
            pair = (2 * n, 2 * n + 1)
            mixed = [jnp.dot(lows[h], values, preferred_element_type=F32) for h in pair]
            dq = [jnp.dot(grads[h], keys, preferred_element_type=F32) for h in pair]
            dk_ref[keys_at, group] += sum(tn_dot(grads[h], heads[h][1]) for h in pair)
            dv_ref[keys_at, group] += sum(tn_dot(lows[h], heads[h][2]) for h in pair)
            out_ref[rows, group] = jnp.where(first, mixed[0], mixed[1]).astype(BF16)
            turned = jnp.where(first, dq[0], dq[1]) * SCALING
            out_ref[rows, pl.ds(embed + n * LANES, LANES)] = unturn(
                turned, cos_ref[rows, :], sin_ref[rows, :]
            ).astype(BF16)

    for n, count in enumerate(sizes):

        @pl.when(variant_ref[at] == n)
        def _(count=count):
            block(count)

    @pl.when(at == pl.num_programs(0) - 1)
    def _():
        for n, group in enumerate(groups):
            out_ref[:, pl.ds(2 * embed + n * LANES, LANES)] = unturn(
                dk_ref[:, group], cos_ref[...], sin_ref[...]
            ).astype(BF16)
            out_ref[:, pl.ds(3 * embed + n * LANES, LANES)] = dv_ref[:, group].astype(BF16)


def attend(qkv, g, starts, cos, sin, after=()):
    extent, embed = g.shape
    span = min(256, extent)
    spans = extent // span
    sizes = [size for size in range(1, spans) if size <= 4 or size % 2 == 0] + [spans]
    heads = starts.reshape(spans, span)[:, 0]
    need = jnp.arange(spans, dtype=jnp.int32) - heads // span + 1
    variant = jnp.sum((need[:, None] > jnp.asarray(sizes, jnp.int32)[None, :]).astype(jnp.int32), axis=1)
    spec = pl.BlockSpec
    return pl.pallas_call(
        behind(partial(attend_kernel, tuple(sizes)), 7, after, 1),
        grid_spec=pltpu.PrefetchScalarGridSpec(
            num_scalar_prefetch=1,
            grid=(spans,),
            in_specs=[
                spec((span, embed), lambda i, s: (i, 0)),
                spec((extent, embed), lambda i, s: (0, 1)),
                spec((extent, embed), lambda i, s: (0, 2)),
                spec((span, embed), lambda i, s: (i, 0)),
                spec((span, 1), lambda i, s: (i, 0)),
                spec((extent, LANES), lambda i, s: (0, 0)),
                spec((extent, LANES), lambda i, s: (0, 0)),
                *unused(after),
            ],
            out_specs=spec((extent, 4 * embed), lambda i, s: (0, 0)),
            scratch_shapes=[pltpu.VMEM((extent, embed), F32), pltpu.VMEM((extent, embed), F32)],
        ),
        out_shape=jax.ShapeDtypeStruct((extent, 4 * embed), BF16),
        compiler_params=params(),
        cost_estimate=work(12 * embed * extent * extent, extent * embed * 16),
        name="attend",
    )(variant, qkv, qkv, qkv, g, starts[:, None], cos, sin, *after)


def dense_back_kernel(
    back_ref, inner_ref, branch_ref, x_ref, stat_ref, gain_ref, wqkv_ref, win_ref, wo_ref,
    out_ref, feature_ref, sums_ref,
):
    parts, rows, part = x_ref.shape
    extra = sums_ref.shape[0]
    total_rows = (out_ref.shape[1] - extra) // 2
    embed = wo_ref.shape[0]
    step = pl.program_id(0)
    mean, inverse = stat_ref[:, 0:1], stat_ref[:, 1:2]

    @pl.when(step == 0)
    def _():
        feature_ref[...] = jnp.zeros_like(feature_ref)
        sums_ref[...] = jnp.zeros_like(sums_ref)

    first = pl.ds(pl.multiple_of(step * rows, rows), rows)
    second = pl.ds(pl.multiple_of(total_rows + step * rows, rows), rows)
    ones = jnp.ones((8, LANES), BF16)
    one = two = None
    for k in range(parts):
        at = pl.ds(k * part, part)
        total = jnp.dot(inner_ref[...], win_ref[:, at], preferred_element_type=F32)
        total += jnp.dot(
            back_ref[:, pl.ds(embed, 3 * embed)], wqkv_ref[:, at], preferred_element_type=F32
        )
        out_ref[k, first, :] = total.astype(BF16)
        out_ref[k, second, :] = (
            jnp.dot(back_ref[:, pl.ds(0, embed)], wo_ref[:, at], preferred_element_type=F32)
            + branch_ref[:, at].astype(F32)
        ).astype(BF16)
        scaled = (x_ref[k].astype(F32) - mean) * inverse
        product = total * scaled
        feature_ref[0:1, at] += jnp.sum(product, axis=0, keepdims=True)
        feature_ref[1:2, at] += jnp.sum(total, axis=0, keepdims=True)
        gain = gain_ref[:, at]
        for n in range(part // LANES):
            lanes = slice(n * LANES, (n + 1) * LANES)
            gained, moved = total[:, lanes] * gain[:, lanes], product[:, lanes] * gain[:, lanes]
            one = gained if one is None else one + gained
            two = moved if two is None else two + moved
    one, two = (
        lax.dot_general(ones, sums.astype(BF16), NT, preferred_element_type=F32) for sums in (one, two)
    )
    pieces = max(rows // part, 1)
    for start, row in ((0, one), (total_rows // part, two)):
        for n in range(pieces):
            sums_ref[pl.ds(start + step * pieces + n, 1), :] = row[0:1, n * part : (n + 1) * part]

    @pl.when(step == pl.num_programs(0) - 1)
    def _():
        for k in range(parts):
            out_ref[k, pl.ds(2 * total_rows, extra), :] = sums_ref[...].astype(BF16)


def extra_rows(total, part):
    return -(-2 * total // part // 16) * 16


def dense_back(back, inner_grad, branch, x, stat, gain, wqkv, win, wo, after=()):
    parts, total, part = x.shape
    embed, width = wo.shape
    inner = win.shape[0]
    rows = min(512, total)
    extra = extra_rows(total, part)
    whole = lambda i: (0, 0)
    block = lambda i: (i, 0)
    return pl.pallas_call(
        behind(dense_back_kernel, 9, after),
        grid=(total // rows,),
        in_specs=[
            pl.BlockSpec((rows, 4 * embed), block),
            pl.BlockSpec((rows, inner), block),
            pl.BlockSpec((rows, width), block),
            pl.BlockSpec((parts, rows, part), lambda i: (0, i, 0)),
            pl.BlockSpec((rows, LANES), block),
            pl.BlockSpec((1, width), whole),
            pl.BlockSpec((3 * embed, width), whole),
            pl.BlockSpec((inner, width), whole),
            pl.BlockSpec((embed, width), whole),
            *unused(after),
        ],
        out_specs=[
            pl.BlockSpec((parts, 2 * total + extra, part), lambda i: (0, 0, 0)),
            pl.BlockSpec((2, width), whole),
        ],
        out_shape=[
            jax.ShapeDtypeStruct((parts, 2 * total + extra, part), BF16),
            jax.ShapeDtypeStruct((2, width), F32),
        ],
        scratch_shapes=[pltpu.VMEM((extra, part), F32)],
        compiler_params=params(),
        cost_estimate=work(2 * total * width * (4 * embed + 2 * inner), total * (6 * width + 8 * embed + 4 * inner)),
        name="dense_back",
    )(back, inner_grad, branch, x, stat, gain, wqkv, win, wo, *after)


def tn_dot(left, right):
    return lax.dot_general(left, right, TN, preferred_element_type=F32)


def piece_rows(shapes, devices):
    return [rows * columns // (devices * LANES) for rows, columns in shapes]


def grads_kernel(chunks, steps, n_in, n_small, make, core_ref, *refs):
    at = chunks * n_in
    ins, small_refs, refs = refs[:at], refs[at : at + n_small], refs[at + n_small :]
    keep_ref, send_ref, *totals = refs
    at = pl.program_id(0)

    @pl.when(at == 0)
    def _():
        for total in totals:
            total[...] = jnp.zeros_like(total)

    for c in range(chunks):

        @pl.when(at // steps == c)
        def _(c=c):
            make(ins[c * n_in : (c + 1) * n_in], totals)

    @pl.when(at == chunks * steps - 1)
    def _():
        chips = keep_ref.shape[0]
        for core, out_ref in ((core_ref[0], keep_ref), (1 - core_ref[0], send_ref)):
            for chip in range(chips):
                offset = 0
                for total in (*totals, *small_refs):
                    rows = total.shape[0] // (2 * chips)
                    start = pl.multiple_of((core * chips + chip) * rows, rows)
                    for n in range(total.shape[1] // LANES):
                        out_ref[chip, pl.ds(offset, rows), :] = total[
                            pl.ds(start, rows), pl.ds(n * LANES, LANES)
                        ].astype(BF16)
                        offset += rows


def feed_make(ins, totals):
    act, hidden, inner_grad, cot = ins
    outer_total, inner_total = totals
    parts, _, part = cot.shape
    left = act[...]
    for k in range(parts):
        outer_total[:, pl.ds(k * part, part)] += tn_dot(left, cot[k])
    inner_total[...] += tn_dot(hidden[...], inner_grad[...])


def head_make(ins, totals):
    back, hidden, cot = ins
    output_total, *projection_totals = totals
    parts, _, part = cot.shape
    embed = output_total.shape[0]
    left = back[:, pl.ds(0, embed)]
    for k in range(parts):
        output_total[:, pl.ds(k * part, part)] += tn_dot(left, cot[k])
    for n, total in enumerate(projection_totals):
        total[...] += tn_dot(hidden[...], back[:, pl.ds((n + 1) * embed, embed)])


def grads(make, shapes, name, core, devices, chunk_arrays, small=(), after=(), times=3):
    chunks = len(chunk_arrays)
    total = chunk_arrays[0][0].shape[0]
    rows = min(512, total)
    steps = total // rows
    specs, arrays = [], []
    for c, group in enumerate(chunk_arrays):
        pick = lambda i, c=c: jnp.clip(i - c * steps, 0, steps - 1)
        for array in group:
            if array.ndim == 2:
                specs.append(pl.BlockSpec((rows, array.shape[1]), lambda i, s, pick=pick: (pick(i), 0)))
            else:
                specs.append(
                    pl.BlockSpec((array.shape[0], rows, array.shape[2]), lambda i, s, pick=pick: (0, pick(i), 0))
                )
            arrays.append(array)
    for array in small:
        specs.append(pl.BlockSpec(array.shape, lambda i, s: (0, 0)))
        arrays.append(array)
    packed = (devices // 2, sum(piece_rows((*shapes, *[a.shape for a in small]), devices)), LANES)
    kernel = partial(grads_kernel, chunks, steps, len(chunk_arrays[0]), len(small), make)
    return pl.pallas_call(
        behind(kernel, len(specs), after, 1),
        grid_spec=pltpu.PrefetchScalarGridSpec(
            num_scalar_prefetch=1,
            grid=(chunks * steps,),
            in_specs=specs + unused(after),
            out_specs=[pl.BlockSpec(packed, lambda i, s: (0, 0, 0))] * 2,
            scratch_shapes=[pltpu.VMEM(shape, F32) for shape in shapes],
        ),
        out_shape=[jax.ShapeDtypeStruct(packed, BF16)] * 2,
        compiler_params=params(),
        cost_estimate=work(
            sum(2 * chunks * total * a * b for a, b in shapes), 2 * sum(a.size for a in arrays), times
        ),
        name=name,
    )(core, *arrays, *after)


def fold_kernel(*refs):
    for n in range(refs[-1].shape[0]):
        refs[-1][n] = sum(ref[n].astype(F32) for ref in refs[:-1]).astype(BF16)


def elementwise(kernel, name, arrays, shape=None, after=()):
    spec = pl.BlockSpec(memory_space=pltpu.VMEM)
    shape = arrays[0].shape if shape is None else shape
    return pl.pallas_call(
        behind(kernel, len(arrays), after),
        in_specs=[spec] * len(arrays) + unused(after),
        out_specs=spec,
        out_shape=jax.ShapeDtypeStruct(shape, BF16),
        compiler_params=params(),
        cost_estimate=work(3 * arrays[0].size, 6 * arrays[0].size),
        name=name,
    )(*arrays, *after)


def merge_kernel(pieces_ref, keep_ref, came_ref, out_ref):
    rows = pieces_ref.shape[1]
    total = pieces_ref[0].astype(F32)
    for n in range(1, pieces_ref.shape[0]):
        total += pieces_ref[n].astype(F32)
    total = total.astype(BF16)
    for n in range(out_ref.shape[0]):
        out_ref[n, pl.ds(0, rows), :] = total
        out_ref[n, pl.ds(rows, keep_ref.shape[1]), :] = (
            keep_ref[n].astype(F32) + came_ref[n].astype(F32)
        ).astype(BF16)


def add_kernel(skip, x_ref, out_ref):
    rows = pl.ds(skip, out_ref.shape[1])
    total = x_ref[0, rows, :].astype(F32)
    for n in range(1, x_ref.shape[0]):
        total += x_ref[n, rows, :].astype(F32)
    total = total.astype(BF16)
    for n in range(out_ref.shape[0]):
        out_ref[n] = total


def passed_on(array, after):
    spec = pl.BlockSpec(memory_space=pl.ANY)
    return pl.pallas_call(
        lambda *refs: None,
        in_specs=[spec] * (1 + len(after)),
        out_specs=spec,
        out_shape=jax.ShapeDtypeStruct(array.shape, array.dtype),
        input_output_aliases={0: 0},
        compiler_params=params(),
        name="passed_on",
    )(array, *after)


def unpack_kernel(n_out, core_ref, own_ref, other_ref, *refs):
    matrix_refs, vector_refs, small_refs = refs[:n_out], refs[n_out:], ()
    if len(refs) > n_out:
        vector_refs, small_refs = refs[n_out:-1], refs[-1:]
    chips = own_ref.shape[0]
    for core, ref in ((core_ref[0], own_ref), (1 - core_ref[0], other_ref)):
        for chip in range(chips):
            offset = 0
            for out_ref in (*matrix_refs, *small_refs):
                rows = out_ref.shape[0] // (2 * chips)
                start = pl.multiple_of((core * chips + chip) * rows, rows)
                for block in range(out_ref.shape[1] // LANES):
                    out_ref[pl.ds(start, rows), pl.ds(block * LANES, LANES)] = ref[
                        chip, pl.ds(offset, rows), :
                    ].astype(F32)
                    offset += rows
    row = 0
    for out_ref in vector_refs:
        for block in range(out_ref.shape[1] // LANES):
            out_ref[:, pl.ds(block * LANES, LANES)] = small_refs[0][pl.ds(row, 1), :]
            row += 1


def unpack(core, own, other, shapes, vectors=(), small_shape=None, after=()):
    spec = pl.BlockSpec(memory_space=pltpu.VMEM)
    outs = (*shapes, *[(1, size) for size in vectors])
    return pl.pallas_call(
        behind(partial(unpack_kernel, len(shapes)), 2, after, 1),
        in_specs=[pl.BlockSpec(memory_space=pltpu.SMEM), spec, spec] + unused(after),
        out_specs=[spec] * len(outs),
        out_shape=[jax.ShapeDtypeStruct(shape, F32) for shape in outs],
        scratch_shapes=[pltpu.VMEM(small_shape, F32)] if vectors else [],
        compiler_params=params(),
        cost_estimate=work(own.size, 12 * own.size),
        name="unpack",
    )(core, own, other, *after)


def last_step_kernel(chunks, width, *refs):
    both_refs, stat_refs, tok_refs, cot_refs = (refs[n * chunks : (n + 1) * chunks] for n in range(4))
    gain_ref, bias_ref, out_ref, grad_ref, plain_ref, columns_ref = refs[4 * chunks :]
    per, span, part = tok_refs[0].shape
    halves = part // LANES
    total = per * LANES
    step = pl.program_id(0)

    @pl.when(step == 0)
    def _():
        for c, both_ref in enumerate(both_refs):
            sums = both_ref[pl.ds(2 * total, both_ref.shape[0] - 2 * total), :]
            shape = (sums.shape[0], LANES)
            eye = lax.broadcasted_iota(jnp.int32, shape, 0) == lax.broadcasted_iota(jnp.int32, shape, 1)
            for h in range(halves):
                columns_ref[c * halves + h] = tn_dot(
                    sums[:, h * LANES : (h + 1) * LANES], eye.astype(F32).astype(BF16)
                ) * (1.0 / width)

    here = pl.ds(pl.multiple_of(step * span, span), span)
    for c, (both_ref, stat_ref, tok_ref, cot_ref) in enumerate(zip(both_refs, stat_refs, tok_refs, cot_refs)):
        for n in range(per):
            r = c * per + n
            at = n * LANES + step * span
            hidden_grad = both_ref[pl.ds(pl.multiple_of(at, span), span), :].astype(F32)
            branch = both_ref[pl.ds(pl.multiple_of(total + at, span), span), :].astype(F32)
            columns = columns_ref[c * halves + n % halves, here, :]
            first = columns[:, n // halves : n // halves + 1]
            second = columns[:, (per + n) // halves : (per + n) // halves + 1]
            mean, inverse = stat_ref[n, :, 0:1], stat_ref[n, :, 1:2]
            token = tok_ref[n].astype(F32)
            scaled = (token - mean) * inverse
            plain_ref[:, r, :] = token + branch + bias_ref[...]
            grad_ref[:, r, :] = cot_ref[n].astype(F32) + inverse * (
                hidden_grad * gain_ref[...] - first - scaled * second
            )
    out_ref[...] = plain_ref[...].astype(BF16)


def last_step(boths, stats, tokens, cotangents, gain, bias, width, positions):
    chunks = len(boths)
    total, part = tokens[0].shape
    per = total // positions
    rows = chunks * per
    in_rows = lambda array: array.reshape(per, positions, array.shape[1])
    span = min(32, positions)
    return pl.pallas_call(
        partial(last_step_kernel, chunks, width),
        grid=(positions // span,),
        in_specs=[
            *[pl.BlockSpec(both.shape, lambda i: (0, 0)) for both in boths],
            *[pl.BlockSpec((per, span, LANES), lambda i: (0, i, 0))] * chunks,
            *[pl.BlockSpec((per, span, part), lambda i: (0, i, 0))] * (2 * chunks),
            *[pl.BlockSpec((1, part), lambda i: (0, 0))] * 2,
        ],
        out_specs=[pl.BlockSpec((span, rows, part), lambda i: (i, 0, 0))] * 2,
        out_shape=[
            jax.ShapeDtypeStruct((positions, rows, part), BF16),
            jax.ShapeDtypeStruct((positions, rows, part), F32),
        ],
        scratch_shapes=[
            pltpu.VMEM((span, rows, part), F32),
            pltpu.VMEM((chunks * (part // LANES), LANES, LANES), F32),
        ],
        compiler_params=params(),
        cost_estimate=work(20 * total * part, 12 * total * part),
        name="last_step",
    )(*boths, *map(in_rows, (*stats, *tokens, *cotangents)), gain, bias)


def partner(array, axis, bit):
    size = lax.axis_size(axis)
    return lax.ppermute(array, axis, [(i, i ^ bit) for i in range(size)])


def to_chips(pieces, axis):
    size = lax.axis_size(axis)
    groups = [list(range(core, size, 2)) for core in range(2)]
    return lax.all_to_all(pieces, axis, 0, 0, tiled=True, axis_index_groups=groups)


def small_sum(array, axes):
    for axis in axes:
        bit = 1
        while bit < lax.axis_size(axis):
            array = array + partner(array, axis, bit)
            bit *= 2
    return array


def body(
    tokens, norm_gain, norm_shift, query_weight, key_weight, value_weight, output_weight,
    inner_weight, inner_bias, outer_weight, outer_bias, lengths, cotangent,
):
    shard_len, batch_rows, local_width = tokens.shape
    seq_count, tp_count = lax.axis_size("seq"), lax.axis_size("tp")
    position, width_index = lax.axis_index("seq"), lax.axis_index("tp")
    extent = shard_len * seq_count
    width, embed = query_weight.shape
    inner = inner_weight.shape[1]
    chunks = batch_rows // seq_count

    own_tokens, own_cotangent = (
        [jnp.swapaxes(part, 0, 1).reshape(extent, local_width) for part in jnp.split(array, chunks, axis=1)]
        for array in (tokens, cotangent)
    )
    back_qkv = jnp.concatenate([w.T for w in (query_weight, key_weight, value_weight)], axis=0)
    back_inner, back_output, back_outer = inner_weight.T, output_weight.T, outer_weight.T
    token_parts = [lax.all_gather(own_tokens[c], "tp") for c in range(chunks)]
    cotangent_parts = [lax.all_gather(own_cotangent[c], "tp") for c in range(chunks)]
    vectors = lax.all_gather(jnp.stack([norm_gain, norm_shift]), "tp", axis=1, tiled=True)
    vectors = vectors.astype(F32)
    gain, shift = vectors[0:1], vectors[1:2]

    starts, places = packing(lengths, extent)
    own_places = lax.dynamic_slice_in_dim(places, position * shard_len, shard_len, 1)
    own_cos, own_sin = turn_tables(own_places.reshape(chunks, extent))
    row_starts = [lax.dynamic_index_in_dim(starts, c * seq_count + position, 0, False) for c in range(chunks)]
    row_places = [lax.dynamic_index_in_dim(places, c * seq_count + position, 0, False) for c in range(chunks)]
    row_tables = [turn_tables(row) for row in row_places]
    bias_row = inner_bias.astype(F32)[None]

    def exchange(array):
        split = array.reshape(seq_count, shard_len, array.shape[-1])
        return lax.all_to_all(split, "seq", 0, 0, tiled=True).reshape(extent, array.shape[-1])

    stages = [dict() for _ in range(chunks)]
    place = jnp.stack([position % 2, position // 2]).astype(jnp.int32)
    feed_shapes = ((inner, width), (width, inner))

    def project(c, after=()):
        o = stages[c]
        o["hidden"], qkv, o["act"], o["slope"], o["stat"], o["branch"] = norm_project(
            token_parts[c], gain, shift, query_weight, key_weight, value_weight, inner_weight,
            bias_row, outer_weight, own_cos[c], own_sin[c], after=after,
        )
        o["qkv_rows"] = exchange(qkv)

    def push(c, after=()):
        o = stages[c]
        mixed_grad, o["inner_grad"], o["bias"] = push_back(
            cotangent_parts[c], back_output, back_outer, o["slope"], after=after, times=20 if c else 3
        )
        o["grad_rows"] = exchange(mixed_grad)

    def feed_grads(c):
        o = stages[c]
        keep, send = grads(
            feed_make, feed_shapes, "feed_grads", place[:1], seq_count,
            [(o["act"], o["hidden"], o["inner_grad"], cotangent_parts[c])],
        )
        return keep, partner(send, "seq", 1)

    def mix(c, after=()):
        o = stages[c]
        o["attention"] = attend(o["qkv_rows"], o["grad_rows"], row_starts[c], *row_tables[c], after=after)
        o["back"] = exchange(o["attention"])

    def finish(c, after=()):
        o = stages[c]
        o["made"], o["feature"] = dense_back(
            o["back"], o["inner_grad"], o["branch"], token_parts[c], o["stat"], gain, back_qkv, back_inner,
            output_weight, after=after,
        )
        o["both"] = lax.psum_scatter(o["made"], "tp", scatter_dimension=0)

    feed = []
    for c in range(chunks):
        if c == 0:
            project(c)
            push(c, after=(stages[c]["qkv_rows"], back_qkv, back_inner))
        else:
            project(c, after=(stages[c - 1]["attention"],))
            finish(c - 1, after=(stages[c]["hidden"],))
            push(c, after=(stages[c - 1]["made"], stages[c]["qkv_rows"]))
        feed.extend(feed_grads(c))
        mix(c, after=(feed[-2],))
    outs = stages

    def both(make):
        return sum(make(c, outs[c]) for c in range(chunks))

    last = stages[-1]
    feed = elementwise(fold_kernel, "fold", feed, after=(last["attention"],))
    finish(chunks - 1, after=(feed,))
    feed = to_chips(feed, "seq")

    feature = small_sum(both(lambda c, o: o["feature"]).reshape(-1, LANES), ("tp",)).reshape(2, width)
    feature = lax.dynamic_slice_in_dim(feature, width_index * local_width, local_width, 1)
    small = jnp.concatenate(
        [
            feature.reshape(-1), both(lambda c, o: o["bias"])[0],
            jnp.sum(cotangent.astype(F32), axis=(0, 1)),
        ]
    )
    small_shape = (seq_count * 16, LANES)
    small = jnp.pad(small, (0, small_shape[0] * LANES - small.size)).reshape(small_shape)
    head_shapes = ((embed, width), (width, embed), (width, embed), (width, embed))
    heads = grads(
        head_make, head_shapes, "head_grads", place[:1], seq_count,
        [(o["back"], o["hidden"], cotangent_parts[c]) for c, o in enumerate(stages)],
        small=(small,), after=(last["made"],), times=0,
    )
    merged = elementwise(
        merge_kernel, "merge", [feed, heads[0], partner(heads[1], "seq", 1)],
        (feed.shape[0], feed.shape[1] + heads[0].shape[1], LANES),
    )
    merged = to_chips(merged, "seq")
    outer_grad, inner_wgrad = unpack(
        place[:1], merged, partner(merged, "seq", 1), feed_shapes, after=tuple(o["both"] for o in stages[:-1])
    )
    heads = elementwise(partial(add_kernel, feed.shape[1]), "add_up", [merged], heads[0].shape)
    heads = to_chips(heads, "seq")

    layer_out, token_grad = last_step(
        [o["both"] for o in outs], [o["stat"] for o in outs], own_tokens, own_cotangent,
        norm_gain.astype(F32)[None], outer_bias.astype(F32)[None], width, shard_len,
    )
    heads = passed_on(heads, (outer_grad, layer_out, token_grad))
    output_grad, query_grad, key_grad, value_grad, *vectors = unpack(
        place[:1], heads, partner(heads, "seq", 1), head_shapes,
        vectors=(local_width, local_width, inner, local_width), small_shape=small_shape,
    )
    gain_grad, shift_grad, inner_bias_grad, outer_bias_grad = (v.reshape(-1) for v in vectors)
    return (
        layer_out, token_grad, gain_grad, shift_grad, query_grad, key_grad, value_grad, output_grad, inner_wgrad,
        inner_bias_grad, outer_grad, outer_bias_grad,
    )


def solution(mesh):
    return jax.shard_map(
        body,
        mesh=mesh,
        in_specs=(
            P("seq", None, "tp"), P("tp"), P("tp"), P(None, "tp"), P(None, "tp"), P(None, "tp"),
            P("tp", None), P(None, "tp"), P("tp"), P("tp", None), P("tp"), P(), P("seq", None, "tp"),
        ),
        out_specs=(
            P("seq", None, "tp"), P("seq", None, "tp"), P("tp"), P("tp"), P(None, "tp"), P(None, "tp"),
            P(None, "tp"), P("tp", None), P(None, "tp"), P("tp"), P("tp", None), P("tp"),
        ),
        check_vma=False,
    )
```
